32 devices in a mesh: atm: 8 (over y, x, core), ocn: 4 (over z).
Axes of the slice: x: 2, y: 2, z: 4, core: 2. Of those that a mesh axis runs over, the one named last changes fastest.
Arguments:
- atm_state: float32 [6912, 3, 512], P('atm', None, 'ocn'), may hold values from -6 to 6
- diffusivity: float32 [6912, 3, 512], P('atm', None, 'ocn'), may hold values from 0.1 to 0.24
- ocean_state: float32 [8192, 3, 128], P(('atm', 'ocn')), may hold values from -6 to 6
- land_mask: int32 [8192, 128], P(('atm', 'ocn')), may hold values 0 or 1
- intersection_area: float32 [16384, 128], P(('atm', 'ocn')), may hold values from 0.2 to 1
- intersection_seg: int32 [16384], P(('atm', 'ocn')), may hold values from 0 to 255
- intersection_dest: int32 [16384, 1], P(('atm', 'ocn')), may hold values from 0 to 31; in each aligned block of 512 rows (0 to 511, 512 to 1023, ...) at most 32 rows name the same one
- intersection_row: int32 [16384], P(('atm', 'ocn')), may hold values from 0 to 863
Outputs:
- atm_next: float32 [6912, 3, 512], P('atm', None, 'ocn')
- ocean_flux: float32 [8192, 3, 128], P(('atm', 'ocn'))
The draws below stay inside these ranges and needn't reach their ends.
Inputs may be any that keep to these rules, and one draw needn't show every extreme that they name: intersection_seg indexes the segments owned by the same device as the intersection row. `intersection_dest`: among the 512 intersection rows of one device, no device is named by more than 32 rows, and some device is named by exactly 32.
All inputs are finite; a program needn't handle non-finite values. No bound on the sum of `land_mask` on one device may be relied on, other than what follows from the above.
Results may differ from the reference program's by a relative error of at most 0.00002.
Values sent between devices are 32-bit elements; how exact they have to be, the bound alone decides.
No kernel may reach another device: no remote copies, remote signals or barrier semaphores. Data moves between devices by JAX's collectives and lax.ppermute only.
A program may use at most 64 MiB of HBM per device.

```python
import math
import jax
import jax.numpy as jnp
import numpy as np

BY = 864
SEG_W = 128
SEG_DEV = 256
ITERS = 3
OV_DEV = 512
CAP = 32
AY = 6912
AX = 512
NSEG = 8192
NOV = 16384
N_ATM = 8
N_OCN = 4
DEVICES = 32


def place_ends(entries, own_key, least, high):
    index_at = [jax.random.randint(jax.random.fold_in(own_key, axis), (), 0, length) for axis, length in enumerate(entries.shape)]
    longest = entries.shape.index(max(entries.shape))
    next_to = index_at[:longest] + [(index_at[longest] + 1) % entries.shape[longest]] + index_at[longest + 1:]
    return entries.at[tuple(index_at)].set(least).at[tuple(next_to)].set(high)


def level_of(key, extent, shards, low, largest):
    def one(axis_at, shards_of):
        heights = jax.random.uniform(jax.random.fold_in(jax.random.fold_in(key, 6), axis_at), (shards_of,), jnp.float32, low / len(shards), largest / len(shards))
        return jnp.repeat(jnp.exp(heights), extent[axis_at] // shards_of).reshape((-1,) + (1,) * (len(extent) - axis_at - 1))

    level = one(*shards[0])
    for cut in shards[1:]:
        level = level * one(*cut)
    return level


def routed_block(rng, own, number, rows, count, top, limit, skew):
    ranking = jax.random.permutation(rng, count)
    packed, ordinary = shares(count, rows * top, limit, skew, True), shares(count, rows * top, limit, skew, False)
    places = jnp.arange(count)

    def named(lengths, offset_by):
        used = int((lengths > 0).sum())
        fixed = max(1, used // 4)
        moved = fixed + (places - fixed + offset_by * (used - fixed)) % max(1, count - fixed)
        return jnp.zeros((count,), jnp.int32).at[ranking[jnp.where(places < fixed, places, moved)]].set(jnp.asarray(lengths, jnp.int32))

    lengths = jnp.where(number % 4 == 0, named(packed, number // 4), named(ordinary, number - number // 4 - 1))
    mixed = jax.random.permutation(jax.random.fold_in(own, 3), count)
    source_of, taker = mixed[0:count // 2 * 2:2], mixed[1:count // 2 * 2:2]
    slack = jnp.minimum(lengths[source_of] - 1, limit - lengths[taker]) // 2
    slack = jnp.where((source_of == ranking[0]) | (taker == ranking[0]) | (lengths[taker] == 0), 0, jnp.maximum(slack, 0))
    moved = jax.random.randint(jax.random.fold_in(own, 4), (count // 2,), 0, 1 << 20) % (slack + 1)
    lengths = lengths.at[source_of].add(-moved).at[taker].add(moved)
    labels = jnp.searchsorted(jnp.cumsum(lengths), jnp.arange(rows * top), side="right").astype(jnp.int32)
    listing = labels.reshape(top, rows).T
    listing = listing[jax.random.permutation(jax.random.fold_in(own, 1), rows)]
    offset_by = jax.random.randint(jax.random.fold_in(own, 2), (rows, 1), 0, top)
    return jnp.take_along_axis(listing, (jnp.arange(top)[None, :] + offset_by) % top, axis=1)


def shares(number_of, total, reach, skew, full):
    loads = [(1 << 20) // math.isqrt(grade ** skew) + 1 for grade in range(1, number_of + 1)]
    largest = reach if full else min(reach, max(-(-total // number_of), total * loads[0] // sum(loads)))
    least = 1 if total - largest >= number_of - 1 else 0
    counts, surplus = [largest] + [least] * (number_of - 1), total - largest - least * (number_of - 1)
    while surplus > 0:
        candidates = [i for i in range(1, number_of) if counts[i] < largest] or [i for i in range(1, number_of) if counts[i] < reach]
        pool, left = sum([loads[i] for i in candidates]), surplus
        for i in candidates:
            addition = min(reach - counts[i], max(1, left * loads[i] // pool), surplus)
            counts[i] = counts[i] + addition
            surplus = surplus - addition
    return np.array(counts)


def normal_values(own_key, shape, deviation, most, pieces=(), kind=jnp.bfloat16):
    result = deviation * jax.random.normal(own_key, shape, jnp.float32)
    if pieces:
        result = result * level_of(own_key, shape, pieces, -0.22, 0.18)
    return jnp.clip(result, -most, most).astype(kind)


def setup_inputs(seed: int = 0) -> dict:
    streams_of = jax.random.split(jax.random.key(seed), 9)
    atm_state = normal_values(streams_of[0], (AY, 3, AX), 1.0, 6.0, ((0, 8), (2, 4)), jnp.float32)
    diffusivity = jnp.clip(jnp.exp(math.log(0.24) - 0.8754687 * jax.random.uniform(streams_of[1], (AY, 3, AX), jnp.float32) ** level_of(streams_of[1], (AY, 3, AX), ((0, 8), (2, 4)), -0.2, 0.2)), 0.1, 0.24)
    ocean_state = normal_values(streams_of[2], (NSEG, 3, SEG_W), 1.0, 6.0, ((0, 32),), jnp.float32)
    land_mask = place_ends((jax.random.randint(streams_of[3], (NSEG, SEG_W), 0, 4) < 3).astype(jnp.int32), jax.random.fold_in(streams_of[3], 1), 0, 1)
    intersection_area = jnp.clip(0.2 + 0.8 * jax.random.uniform(streams_of[4], (NOV, SEG_W), jnp.float32) ** level_of(streams_of[4], (NOV, SEG_W), ((0, 32),), -0.2, 0.2), 0.2, 1.0)
    intersection_seg = place_ends(jax.random.randint(streams_of[5], (NOV,), 0, SEG_DEV), jax.random.fold_in(streams_of[5], 1), 0, SEG_DEV - 1).astype(jnp.int32)
    intersection_dest_keys = jax.random.split(jax.random.fold_in(streams_of[6], 1), NOV // OV_DEV)
    intersection_dest_turns = jax.random.permutation(jax.random.fold_in(streams_of[6], 3), NOV // OV_DEV)
    intersection_dest = jax.vmap(lambda own, number: routed_block(jax.random.fold_in(streams_of[6], 2), own, number, OV_DEV, DEVICES, 1, CAP, 2))(intersection_dest_keys, intersection_dest_turns).reshape((NOV, 1))
    intersection_row = place_ends(jax.random.randint(streams_of[7], (NOV,), 0, BY), jax.random.fold_in(streams_of[7], 1), 0, BY - 1).astype(jnp.int32)
    return dict(atm_state=atm_state, diffusivity=diffusivity, ocean_state=ocean_state, land_mask=land_mask, intersection_area=intersection_area, intersection_seg=intersection_seg, intersection_dest=intersection_dest, intersection_row=intersection_row)


def neighbours(grid_field):
    padded = jnp.pad(grid_field, ((1, 1), (0, 0), (1, 1)))
    return padded[2:, :, 1:-1] + padded[:-2, :, 1:-1] + padded[1:-1, :, 2:] + padded[1:-1, :, :-2]

def fluxes(ocean_part, air_part):
    wind_east = air_part[:, 1] - ocean_part[:, 1]
    wind_north = air_part[:, 2] - ocean_part[:, 2]
    wind_speed = jnp.sqrt(wind_east * wind_east + wind_north * wind_north + 0.5)
    temp_gap = ocean_part[:, 0] - air_part[:, 0]
    factor = 1.0 + 0.5 * jnp.tanh(temp_gap / wind_speed)
    return jnp.stack([0.8 * factor * wind_speed * temp_gap, 0.6 * factor * wind_speed * wind_east, 0.6 * factor * wind_speed * wind_north], axis=1)

def reference(atm_state, diffusivity, ocean_state, land_mask, intersection_area, intersection_seg, intersection_dest, intersection_row):
    dev_count = N_ATM * N_OCN
    smoothed = 0.5 * atm_state + 0.125 * neighbours(atm_state)
    blocks = smoothed.reshape(N_ATM, BY, 3, N_OCN, SEG_W).transpose(0, 3, 1, 2, 4).reshape(dev_count * BY, 3, SEG_W)
    owner_dev = jnp.arange(dev_count * OV_DEV, dtype=jnp.int32) // OV_DEV
    seg_global = (owner_dev * SEG_DEV + intersection_seg).astype(jnp.int32)
    row_global = (intersection_dest[:, 0] * BY + intersection_row).astype(jnp.int32)
    weight = intersection_area * land_mask[seg_global].astype(jnp.float32)
    weighted = weight[:, None, :] * fluxes(ocean_state[seg_global], blocks[row_global])
    ocean_flux = jax.ops.segment_sum(weighted, seg_global, num_segments=dev_count * SEG_DEV)
    air_sum = jax.ops.segment_sum(weighted, row_global, num_segments=dev_count * BY)
    air_sum = air_sum.reshape(N_ATM, N_OCN, BY, 3, SEG_W).transpose(0, 2, 3, 1, 4).reshape(N_ATM * BY, 3, N_OCN * SEG_W)
    direction_sign = jnp.array([1.0, -1.0, -1.0], dtype=jnp.float32)[None, :, None]
    current = atm_state + direction_sign * air_sum
    for iteration in range(ITERS):
        current = current + diffusivity * (neighbours(current) - 4.0 * current)
    return (current, ocean_flux)
```

```python
import functools

import jax
import jax.numpy as jnp
from jax import lax
from jax.experimental import pallas as pl
from jax.experimental.pallas import tpu as pltpu
from jax.sharding import PartitionSpec as P

ITERS = 3
EDGE = 8
FLAT = 32
STRIP = 6 * ITERS
BOTH = ("atm", "ocn")
F32 = jnp.float32
BF16 = jnp.bfloat16


def split3(x):
    high = x.astype(BF16)
    rest = x - high.astype(F32)
    middle = rest.astype(BF16)
    low = (rest - middle.astype(F32)).astype(BF16)
    return high, middle, low


def dot(a, b, contract=(1, 0)):
    dims = (((contract[0],), (contract[1],)), ((), ()))
    return lax.dot_general(a, b, dims, preferred_element_type=F32)


def exact_dots(select, values, contract=(1, 0)):
    parts = [split3(x) for x in values]
    stacked = jnp.concatenate([p[level] for level in (2, 1, 0) for p in parts], axis=1)
    width, count = values[0].shape[1], len(values)
    result = dot(select, stacked, contract)

    def piece(level, index):
        at = (level * count + index) * width
        return result[:, at : at + width]

    return [(piece(0, i) + piece(1, i)) + piece(2, i) for i in range(count)]


def iota(shape, dim):
    return lax.broadcasted_iota(jnp.int32, shape, dim)


def one_hot(condition):
    return condition.astype(F32).astype(BF16)


class Late:
    def __init__(self, source, target, sem):
        self.target, self.copy = target, pltpu.make_async_copy(source, target, sem)
        self.copy.start()

    def get(self):
        if self.copy is not None:
            self.copy.wait()
            self.copy = None
        return self.target


def call(kernel, out_shape, operands, *, late=(), outs=None, flops=0, scratch=(), limit=16):
    total = sum(x.size * x.dtype.itemsize for x in operands)
    extra = {} if outs is None else {"out_specs": outs}
    given = [
        pltpu.with_memory_space_constraint(x, pltpu.HBM) if i in late else x
        for i, x in enumerate(operands)
    ]
    results = len(jax.tree.leaves(out_shape))

    def body(*refs):
        ends = len(operands), len(operands) + results, len(operands) + results + len(late)
        inputs, held = list(refs[: ends[0]]), refs[ends[1] : ends[2]]
        rest = refs[ends[2] :]
        if late:
            sems, rest = rest[0], rest[1:]
            for at, i in enumerate(late):
                inputs[i] = Late(inputs[i], held[at], sems.at[at])
        kernel(*inputs, *refs[ends[0] : ends[1]], *rest)

    held = [pltpu.VMEM(operands[i].shape, operands[i].dtype) for i in late]
    held += [pltpu.SemaphoreType.DMA((len(late),))] if late else []
    return pl.pallas_call(
        body,
        out_shape=out_shape,
        in_specs=[
            pl.BlockSpec(memory_space=pltpu.HBM if i in late else pltpu.VMEM)
            for i in range(len(operands))
        ],
        scratch_shapes=held + list(scratch),
        compiler_params=pltpu.CompilerParams(vmem_limit_bytes=limit << 20),
        cost_estimate=pl.CostEstimate(flops=flops, bytes_accessed=2 * total, transcendentals=0),
        **extra,
    )(*given)


def positions(target, devices):
    count = target.shape[1]
    earlier = one_hot(iota((count, count), 0) < iota((count, count), 1))
    match = iota((devices, count), 0) == target
    before = dot(one_hot(match), earlier)
    return jnp.sum(jnp.where(match, before, 0.0), axis=0, keepdims=True).astype(jnp.int32)


def pack_kernel(devices, cap, dest, seg, row, ocean, mask, area, out, staged, out_sems):
    target = dest.get()[...]
    slots = devices * cap
    count = target.shape[1]
    chans, segs, width = ocean.target.shape
    stores = []

    def send(index, size, values):
        piece = pl.ds(index * cap, size)
        staged[:, piece, :] = values.reshape(devices, size, width)
        store = pltpu.make_async_copy(
            staged.at[:, piece, :], out.at[:, piece, :], out_sems.at[index]
        )
        store.start()
        stores.append(store)

    position = positions(target, devices)
    slot = target * cap + position
    place = one_hot(iota((slots, count), 0) == slot)
    member = one_hot(iota((segs, count), 0) == seg.get()[...])
    of_seg = dot(place, member, (1, 1)).astype(BF16)
    values = ocean.get()
    for chan, sent in enumerate(exact_dots(of_seg, [values[chan] for chan in range(chans)])):
        send(chan, cap, sent)
    sea = dot(of_seg, mask.get()[...].astype(F32).astype(BF16))
    (reach,) = exact_dots(place, [area.get()[...]])
    send(chans, cap, reach * sea)
    line = iota((devices * EDGE, count), 0)
    tall = line == target * EDGE + (position & (EDGE - 1))
    flat = line == target * EDGE
    lane = iota((width, count), 0)
    tall_lane = lane == lax.shift_right_logical(position, EDGE.bit_length() - 1)
    flat_lane = lane == position + FLAT
    value = row.get()[...]
    coarse, fine = lax.shift_right_logical(value, 5).astype(F32), (value & 31).astype(F32)
    lanes = jnp.concatenate(
        [
            jnp.concatenate([jnp.where(at, v, 0.0) for at in (tall_lane, flat_lane)], axis=1)
            for v in (coarse, fine)
        ],
        axis=0,
    ).astype(BF16)
    labels = dot(jnp.concatenate([one_hot(tall), one_hot(flat)], axis=1), lanes, (1, 1))
    send(chans + 1, EDGE, labels[:, :width] * 32.0 + labels[:, width:])
    for store in stores:
        store.wait()


def edge_lane(takes, width, high):
    def lane(line):
        at, first = jnp.full(line.shape, -1, jnp.int32), 0
        for index, take in enumerate(takes):
            inside = (line >= first) & (line < first + take)
            start = index * width + (width - take if high else 0)
            at = jnp.where(inside, start + line - first, at)
            first += take
        return at

    return lane


def strip_lane(first, chans, width):
    def lane(line):
        at, place = jnp.full(line.shape, -1, jnp.int32), line % STRIP
        start = (first + line // STRIP) * width
        low = (place >= ITERS) & (place < 3 * ITERS)
        high = (place >= 3 * ITERS) & (place < 5 * ITERS)
        at = jnp.where(low, start + place - ITERS, at)
        at = jnp.where(high, start + width + place - 5 * ITERS, at)
        return jnp.where(line < chans * STRIP, at, -1)

    return lane


def fill_strip(own, left, right, first, chans, take):
    pieces = []
    gap = [jnp.zeros((ITERS - take, own.shape[1]), F32)] if take < ITERS else []
    for chan in range(chans):
        beside = slice(first + chan * take, first + (chan + 1) * take)
        inner = slice(chan * STRIP + ITERS, (chan + 1) * STRIP - ITERS)
        pieces += gap + [left[beside, :], own[inner, :], right[beside, :]] + gap
    pieces.append(jnp.zeros((own.shape[0] - chans * STRIP, own.shape[1]), F32))
    return jnp.concatenate(pieces, axis=0)


def edge_columns(pieces, outputs):
    width = pieces[0][0].shape[1]
    length = outputs[0][0].shape[1]
    tail = length - sum(piece.shape[0] for piece in pieces[0])
    whole = jnp.concatenate(
        [jnp.concatenate([*piece, jnp.zeros((tail, width), F32)], axis=0) for piece in pieces],
        axis=1,
    )
    rows = []
    for ref, lane in outputs:
        shape = (ref.shape[0], whole.shape[1])
        rows.append(iota(shape, 1) == lane(iota(shape, 0)))
    select = one_hot(jnp.concatenate([row.astype(jnp.int32) for row in rows], axis=0) > 0)
    top, middle, bottom = split3(whole)
    edges = dot(select, bottom, (1, 1)) + dot(select, middle, (1, 1))
    edges = edges + dot(select, top, (1, 1))
    first = 0
    for ref, _ in outputs:
        ref[...] = edges[first : first + ref.shape[0]]
        first += ref.shape[0]


def first_columns_kernel(before, after, atm, diff, low, high, own):
    chans, _, width = atm.target.shape
    bodies = [ref.get()[chan] for ref in (atm, diff) for chan in range(chans)]
    takes = [1] * chans + [ITERS - 1] * chans
    pieces = [(before[i], body, after[i]) for i, body in enumerate(bodies)]
    edge_columns(
        pieces,
        [
            (low, edge_lane(takes, width, False)),
            (high, edge_lane(takes, width, True)),
            (own, strip_lane(chans, chans, width)),
        ],
    )


def columns_kernel(before, body, after, low, high, own):
    chans, _, width = body.shape
    pieces = [(before[i], body[i], after[i]) for i in range(chans)]
    edge_columns(
        pieces,
        [
            (low, edge_lane([ITERS] * chans, width, False)),
            (high, edge_lane([ITERS] * chans, width, True)),
            (own, strip_lane(0, chans, width)),
        ],
    )


def beside_rows(x):
    rows = x.shape[0]
    return pltpu.roll(x, rows - 1, 0) + pltpu.roll(x, 1, 0)


def beside_columns(x):
    width = x.shape[1]
    return pltpu.roll(x, width - 1, 1), pltpu.roll(x, 1, 1)


def beside_body(body, side=None):
    rows, width = body.shape
    lane = iota(body.shape, 1)
    east, west = beside_columns(body)
    east = jnp.where(lane == width - 1, 0.0 if side is None else side, east)
    west = jnp.where(lane == 0, 0.0 if side is None else side, west)
    return beside_rows(body) + east + west


def smooth_kernel(cap, before, after, atm, dest, seg, smooth, seg_select, staged, held, sems):
    chans, rows, width = staged.shape
    segs, slots = held.shape
    target = dest.get()[...]
    slot = target * cap + positions(target, slots // cap)
    place = one_hot(iota((slots, target.shape[1]), 0) == slot)
    member = one_hot(iota((segs, target.shape[1]), 0) == seg.get()[...])
    held[...] = dot(member, place, (1, 1)).astype(BF16)
    stores = [pltpu.make_async_copy(held, seg_select, sems.at[0])]
    stores[0].start()
    state = atm.get()
    for chan in range(chans):
        body = jnp.concatenate([before[chan], state[chan], after[chan]], axis=0)
        staged[chan] = (0.5 * body + 0.125 * beside_body(body))[EDGE : EDGE + rows]
    stores.append(pltpu.make_async_copy(staged, smooth, sems.at[1]))
    stores[1].start()
    for store in stores:
        store.wait()


def nearest_columns(left, right, width, chans):
    edges = jnp.concatenate([left[:EDGE, :], right[:EDGE, :]], axis=0)
    shape = (6 * EDGE, chans * width)
    which, lane = iota(shape, 0), iota(shape, 1)
    line = which % (2 * EDGE)
    at = jnp.where(line < EDGE, line * width, (line - EDGE) * width + width - 1)
    select = one_hot((lane == at) & (line % EDGE < chans))
    return dot(jnp.concatenate(split3(edges), axis=0), select, (0, 0))


def flux_kernel(cap, incoming, left, right, smooth, out, label_rows, staged, sems):
    devices, _, width = incoming.shape
    chans, rows, _ = smooth.target.shape
    side = 0.125 * nearest_columns(left, right, width, chans)[EDGE : EDGE + rows]
    label_rows[...] = incoming[:, (chans + 1) * cap, :]
    whole = smooth.get()
    smoothed = jnp.concatenate([whole[chan] for chan in range(chans)], axis=1) + side
    table = jnp.concatenate(split3(smoothed)[::-1], axis=1)
    groups = sems.shape[0]
    each = devices // groups
    stores = []
    for group in range(groups):
        owners = slice(group * each, (group + 1) * each)

        def part(index):
            piece = incoming[owners, index * cap : (index + 1) * cap, :]
            return piece.reshape(each * cap, width)

        labels = incoming[owners, (chans + 1) * cap :, :]
        labels = jnp.concatenate(
            [labels[i, :, j : j + 1] for i in range(each) for j in range(cap // EDGE)], axis=0
        ).astype(jnp.int32)
        select = one_hot(iota((each * cap, rows), 1) == labels)
        found = dot(select, table)
        pieces = [found[:, i * width : (i + 1) * width] for i in range(3 * chans)]
        air = [
            (pieces[i] + pieces[chans + i]) + pieces[2 * chans + i] for i in range(chans)
        ]
        wind_east = air[1] - part(1)
        wind_north = air[2] - part(2)
        wind_speed = jnp.sqrt(wind_east * wind_east + wind_north * wind_north + 0.5)
        temp_gap = part(0) - air[0]
        factor = 1.0 + 0.5 * jnp.tanh(temp_gap / wind_speed)
        common = part(3) * factor * wind_speed
        for index, value in enumerate((0.8 * temp_gap, 0.6 * wind_east, 0.6 * wind_north)):
            staged[owners, index * cap : (index + 1) * cap, :] = (common * value).reshape(
                each, cap, width
            )
        store = pltpu.make_async_copy(
            staged.at[pl.ds(group * each, each)],
            out.at[pl.ds(group * each, each)],
            sems.at[group],
        )
        store.start()
        stores.append(store)
    for store in stores:
        store.wait()


def forced_kernel(cap, label_rows, weighted, atm, forced, top, bottom):
    devices, _, width = weighted.target.shape
    chans, rows, _ = forced.shape
    slots = devices * cap
    log = cap.bit_length() - 1
    labels = label_rows[...].astype(jnp.int32)
    spread = one_hot(iota((width, slots), 0) == (iota((width, slots), 1) & (cap - 1)) + FLAT)
    coarse = dot(lax.shift_right_logical(labels, 5).astype(F32).astype(BF16), spread)
    fine = dot((labels & 31).astype(F32).astype(BF16), spread)
    owner = lax.shift_right_logical(iota((devices, slots), 1), log)
    label = jnp.where(owner == iota((devices, slots), 0), coarse * 32.0 + fine, 0.0)
    label = jnp.sum(label, axis=0, keepdims=True).astype(jnp.int32)
    select = one_hot(iota((rows, slots), 0) == label)
    sent, state = weighted.get(), atm.get()
    values = [
        sent[:, chan * cap : (chan + 1) * cap, :].reshape(slots, width) for chan in range(chans)
    ]
    for chan, air_sum in enumerate(exact_dots(select, values)):
        result = state[chan] + air_sum if chan == 0 else state[chan] - air_sum
        forced[chan] = result
        top[chan] = result[:EDGE]
        bottom[chan] = result[-EDGE:]


def diffuse_kernel(
    forced, before, after, diff_own, diff_left, diff_right, diff_before, diff_after, diff,
    out, diff_strip,
):
    chans, rows, width = forced.shape
    diff_strip[...] = fill_strip(diff_own, diff_left, diff_right, chans, chans, ITERS - 1)
    for chan in range(chans):
        body = jnp.concatenate([before[chan], forced[chan], after[chan]], axis=0)
        body_diff = [diff_before[chans + chan], diff.get()[chan], diff_after[chans + chan]]
        body_diff = jnp.concatenate(body_diff, axis=0)
        for _ in range(ITERS):
            body = body + body_diff * (beside_body(body) - 4.0 * body)
        out[chan] = body[EDGE : EDGE + rows]


def sides_kernel(inner, own, left, right, diff_strip, out):
    chans, rows, width = inner.shape
    state = fill_strip(own, left, right, 0, chans, ITERS)
    spread = diff_strip[...]
    for _ in range(ITERS):
        east, west = beside_columns(state)
        state = state + spread * ((beside_rows(state) + east + west) - 4.0 * state)
    lines = state.shape[0]
    shape = (3 * lines, chans * width)
    which, lane = iota(shape, 0) % lines, iota(shape, 1)
    place, start = which % STRIP, which // STRIP * width
    low = (place >= ITERS) & (place < 2 * ITERS) & (lane == start + place - ITERS)
    high = place >= 4 * ITERS
    high = high & (place < 5 * ITERS) & (lane == start + width + place - 5 * ITERS)
    select = one_hot((which < chans * STRIP) & (low | high))
    edges = dot(jnp.concatenate(split3(state), axis=0), select, (0, 0))
    lane = iota((rows, width), 1)
    outer = (lane < ITERS) | (lane >= width - ITERS)
    for chan in range(chans):
        edge = edges[EDGE : EDGE + rows, chan * width : (chan + 1) * width]
        out[chan] = jnp.where(outer, edge, inner[chan])


def sum_kernel(cap, returned, seg_select, out):
    devices, _, width = returned.shape
    values = [
        returned[:, chan * cap : (chan + 1) * cap, :].reshape(devices * cap, width)
        for chan in range(out.shape[0])
    ]
    for chan, total in enumerate(exact_dots(seg_select.get()[...], values)):
        out[chan] = total


def shift(axis, low_edge, high_edge):
    count = lax.axis_size(axis)
    forward = [(i, i + 1) for i in range(count - 1)]
    backward = [(target, source) for source, target in forward]
    return lax.ppermute(high_edge, axis, forward), lax.ppermute(low_edge, axis, backward)


def per_device(atm, diff, ocean, mask, area, seg, dest, row):
    atm_count, ocn_count = lax.axis_size("atm"), lax.axis_size("ocn")
    devices = atm_count * ocn_count
    rows, chans, width = atm.shape
    count = seg.shape[0]
    segs = ocean.shape[0]
    cap = max(2, 2 * count // devices)
    slots = devices * cap
    atm = jnp.transpose(atm, (1, 0, 2))
    diff = jnp.transpose(diff, (1, 0, 2))
    ocean = jnp.transpose(ocean, (1, 0, 2))

    def shape(*dims, dtype=F32):
        return jax.ShapeDtypeStruct(dims, dtype)

    hbm, fast = pltpu.HBM, pl.BlockSpec(memory_space=pltpu.VMEM)
    slow = pl.BlockSpec(memory_space=hbm)
    dest, seg, row = dest.reshape(1, count), seg.reshape(1, count), row.reshape(1, count)
    packed = (devices, (chans + 1) * cap + EDGE, width)
    given = (dest, seg, row, ocean, mask, area)
    out = call(
        functools.partial(pack_kernel, devices, cap),
        hbm(packed, F32),
        given,
        late=tuple(range(len(given))),
        outs=slow,
        scratch=[pltpu.VMEM(packed, F32), pltpu.SemaphoreType.DMA((chans + 2,))],
        flops=2 * slots * count * (segs + 3 * width) + 6 * slots * segs * chans * width,
    )
    incoming = lax.all_to_all(out, BOTH, split_axis=0, concat_axis=0, tiled=True)

    long = -(-(rows + 2 * EDGE) // 128) * 128

    def lines(columns):
        return shape(-(-columns // EDGE) * EDGE, long)

    first = jnp.concatenate([atm[:, :EDGE], diff[:, :EDGE]], axis=0)
    final = jnp.concatenate([atm[:, -EDGE:], diff[:, -EDGE:]], axis=0)
    before, after = shift("atm", first, final)
    low, high, diff_own = call(
        first_columns_kernel,
        (lines(chans * ITERS), lines(chans * ITERS), lines(chans * STRIP)),
        (before, after, atm, diff),
        late=(2, 3),
        flops=6 * 2 * chans * long * width * 16,
    )
    left, right = shift("ocn", low, high)
    smooth, seg_select = call(
        functools.partial(smooth_kernel, cap),
        (hbm((chans, rows, width), F32), hbm((segs, slots), BF16)),
        (before, after, atm, dest, seg),
        late=(2, 3, 4),
        outs=(slow, slow),
        scratch=[
            pltpu.VMEM((chans, rows, width), F32),
            pltpu.VMEM((segs, slots), BF16),
            pltpu.SemaphoreType.DMA((2,)),
        ],
        flops=100 * rows * chans * width,
    )
    weighted, label_rows = call(
        functools.partial(flux_kernel, cap),
        (hbm((devices, chans * cap, width), F32), shape(devices, width)),
        (incoming, left, right, smooth),
        late=(3,),
        outs=(slow, fast),
        scratch=[
            pltpu.VMEM((devices, chans * cap, width), F32),
            pltpu.SemaphoreType.DMA((4,)),
        ],
        flops=100 * slots * width,
    )
    returned = lax.all_to_all(weighted, BOTH, split_axis=0, concat_axis=0, tiled=True)
    forced, top, bottom = call(
        functools.partial(forced_kernel, cap),
        (
            pltpu.VMEM((chans, rows, width), F32),
            shape(chans, EDGE, width),
            shape(chans, EDGE, width),
        ),
        (label_rows, weighted, atm),
        late=(1, 2),
        flops=6 * slots * rows * chans * width,
    )
    forced_before, forced_after = shift("atm", top, bottom)
    forced_low, forced_high, forced_own = call(
        columns_kernel,
        (lines(chans * ITERS), lines(chans * ITERS), lines(chans * STRIP)),
        (forced_before, forced, forced_after),
        flops=6 * chans * long * width * 16,
    )
    forced_left, forced_right = shift("ocn", forced_low, forced_high)
    inner, diff_strip = call(
        diffuse_kernel,
        (shape(chans, rows, width), lines(chans * STRIP)),
        (forced, forced_before, forced_after, diff_own, left, right, before, after, diff),
        late=(8,),
        flops=100 * chans * rows * width,
    )
    atm_next = call(
        sides_kernel,
        shape(chans, rows, width),
        (inner, forced_own, forced_left, forced_right, diff_strip),
        flops=100 * chans * rows * width,
    )
    ocean_flux = call(
        functools.partial(sum_kernel, cap),
        shape(chans, segs, width),
        (returned, seg_select),
        late=(1,),
        flops=6 * slots * segs * chans * width,
    )
    return jnp.transpose(atm_next, (1, 0, 2)), jnp.transpose(ocean_flux, (1, 0, 2))


def solution(mesh):
    placed = (
        P("atm", None, "ocn"),
        P("atm", None, "ocn"),
        P(BOTH, None, None),
        P(BOTH, None),
        P(BOTH, None),
        P(BOTH),
        P(BOTH, None),
        P(BOTH),
    )
    return jax.shard_map(
        per_device,
        mesh=mesh,
        in_specs=placed,
        out_specs=(P("atm", None, "ocn"), P(BOTH, None, None)),
        check_vma=False,
    )
```

```python
import functools

import jax
import jax.numpy as jnp
from jax import lax
from jax.experimental import pallas as pl
from jax.experimental.pallas import tpu as pltpu
from jax.sharding import PartitionSpec as P

ITERS = 3
EDGE = 8
FLAT = 32
STRIP = 6 * ITERS
COST_SEND = 1 << 10
COST_OWN = 1 << 10
COST_MIRROR = 15 << 20
COST_FIRST = 1 << 10
COST_SMOOTH = 100 << 20
BOTH = ("atm", "ocn")
F32 = jnp.float32
BF16 = jnp.bfloat16


def split3(x):
    high = x.astype(BF16)
    rest = x - high.astype(F32)
    middle = rest.astype(BF16)
    low = (rest - middle.astype(F32)).astype(BF16)
    return high, middle, low


def dot(a, b, contract=(1, 0)):
    dims = (((contract[0],), (contract[1],)), ((), ()))
    return lax.dot_general(a, b, dims, preferred_element_type=F32)


def exact_dots(select, values, contract=(1, 0)):
    parts = [split3(x) for x in values]
    stacked = jnp.concatenate([p[level] for level in (2, 1, 0) for p in parts], axis=1)
    width, count = values[0].shape[1], len(values)
    result = dot(select, stacked, contract)

    def piece(level, index):
        at = (level * count + index) * width
        return result[:, at : at + width]

    return [(piece(0, i) + piece(1, i)) + piece(2, i) for i in range(count)]


def iota(shape, dim):
    return lax.broadcasted_iota(jnp.int32, shape, dim)


def one_hot(condition):
    return condition.astype(F32).astype(BF16)


class Late:
    def __init__(self, source, target, sem):
        self.target, self.copy = target, pltpu.make_async_copy(source, target, sem)
        self.copy.start()

    def get(self):
        if self.copy is not None:
            self.copy.wait()
            self.copy = None
        return self.target


def call(
    kernel, out_shape, operands, *, late=(), plain=(), smem=(), after=(), outs=None, cost=None, scratch=(), aliases={},
):
    total = sum(x.size * x.dtype.itemsize for x in operands)
    extra = {} if outs is None else {"out_specs": outs}
    count = len(operands)
    operands = [*operands, *after]
    unread = range(count, len(operands))
    slow = [*late, *plain, *aliases]
    given = [
        pltpu.with_memory_space_constraint(x, pltpu.HBM) if i in slow else x
        for i, x in enumerate(operands)
    ]
    results = len(jax.tree.leaves(out_shape))

    def body(*refs):
        first, second = len(operands), len(operands) + results
        inputs, held = list(refs[:count]), refs[second : second + len(late)]
        rest = refs[second + len(late) :]
        if late:
            sems, rest = rest[0], rest[1:]
            for at, i in enumerate(late):
                inputs[i] = Late(inputs[i], held[at], sems.at[at])
        kernel(*inputs, *refs[first:second], *rest)

    held = [pltpu.VMEM(operands[i].shape, operands[i].dtype) for i in late]
    held += [pltpu.SemaphoreType.DMA((len(late),))] if late else []

    def space(i):
        if i in unread:
            return pl.ANY
        return pltpu.HBM if i in slow else pltpu.SMEM if i in smem else pltpu.VMEM

    return pl.pallas_call(
        body,
        out_shape=out_shape,
        in_specs=[pl.BlockSpec(memory_space=space(i)) for i in range(len(operands))],
        scratch_shapes=held + list(scratch),
        input_output_aliases=aliases,
        compiler_params=pltpu.CompilerParams(vmem_limit_bytes=16 << 20),
        cost_estimate=pl.CostEstimate(flops=(cost or 0) * 1000, bytes_accessed=cost or total, transcendentals=0),
        **extra,
    )(*given)


def positions(target, devices):
    count = target.shape[1]
    earlier = one_hot(iota((count, count), 0) < iota((count, count), 1))
    match = iota((devices, count), 0) == target
    before = dot(one_hot(match), earlier)
    return jnp.sum(jnp.where(match, before, 0.0), axis=0, keepdims=True).astype(jnp.int32)


def pack(sizes, half, target, seg, value, ocean, weight, out, staged, out_sems):
    devices, ocn_count, cap = sizes
    across = ocn_count // 2
    owners = devices // 2
    slots = owners * cap
    count = target.shape[1]
    chans, (segs, width) = len(ocean), ocean[0].shape
    stores = []

    def send(index, size, values):
        piece = pl.ds(index * cap, size)
        staged[:, piece, :] = values.reshape(owners, size, width)
        store = pltpu.make_async_copy(
            staged.at[:, piece, :], out.at[:, piece, :], out_sems.at[index]
        )
        store.start()
        stores.append(store)

    position = positions(target, devices)
    beside = target % ocn_count
    group = target // ocn_count * across + beside % across
    group = jnp.where(beside // across == half, group, owners)
    slot = group * cap + position
    place = one_hot(iota((slots, count), 0) == slot)
    member = one_hot(iota((segs, count), 0) == seg)
    of_seg = dot(place, member, (1, 1)).astype(BF16)
    for chan, sent in enumerate(exact_dots(of_seg, ocean)):
        send(chan, cap, sent)
    (reach,) = exact_dots(place, [weight])
    send(chans, cap, reach)
    line = iota((owners * EDGE, count), 0)
    tall = line == group * EDGE + (position & (EDGE - 1))
    flat = line == group * EDGE
    lane = iota((width, count), 0)
    tall_lane = lane == lax.shift_right_logical(position, EDGE.bit_length() - 1)
    flat_lane = lane == position + FLAT
    coarse, fine = lax.shift_right_logical(value, 5).astype(F32), (value & 31).astype(F32)
    lanes = jnp.concatenate(
        [
            jnp.concatenate([jnp.where(at, v, 0.0) for at in (tall_lane, flat_lane)], axis=1)
            for v in (coarse, fine)
        ],
        axis=0,
    ).astype(BF16)
    labels = dot(jnp.concatenate([one_hot(tall), one_hot(flat)], axis=1), lanes, (1, 1))
    send(chans + 1, EDGE, labels[:, :width] * 32.0 + labels[:, width:])
    return stores


def send_kernel(ocean, seg, mask, area, dest, row, sent, kept, sems):
    segs, width = mask.target.shape
    count = area.target.shape[0]
    lines = count // width
    chans = ocean.target.shape[0]
    values = ocean.get()
    stores = [
        pltpu.make_async_copy(
            values.at[chan], sent.at[pl.ds(chan * segs, segs), :], sems.at[chan]
        )
        for chan in range(chans)
    ]
    for store in stores:
        store.start()
    found = seg.get()[...]
    member = one_hot(iota((segs, count), 0) == found)
    sea = dot(member, mask.get()[...].astype(F32).astype(BF16), (0, 0))
    kept[:count, :] = area.get()[...] * sea
    flat = [
        index[:, line * width : (line + 1) * width].astype(F32)
        for index in (dest.get()[...], found, row.get()[...])
        for line in range(lines)
    ]
    rest = kept.shape[0] - count - len(flat)
    kept[count:, :] = jnp.concatenate(flat + [jnp.zeros((rest, width), F32)], axis=0)
    target = sent.at[pl.ds(chans * segs, kept.shape[0]), :]
    stores.append(pltpu.make_async_copy(kept, target, sems.at[chans]))
    stores[-1].start()
    for store in stores:
        store.wait()


def pack_kernel(sizes, count, chans, half, sent, out, staged, out_sems):
    given = sent.get() if isinstance(sent, Late) else sent
    width = given.shape[1]
    lines = count // width
    rest = -(-3 * lines // 16) * 16
    segs = (given.shape[0] - count - rest) // chans
    first = chans * segs + count

    def vector(index):
        at = first + index * lines
        pieces = [given[at + line : at + line + 1, :] for line in range(lines)]
        return jnp.concatenate(pieces, axis=1).astype(jnp.int32)

    ocean = [given[chan * segs : (chan + 1) * segs, :] for chan in range(chans)]
    weight = given[chans * segs : first, :]
    indices = [vector(index) for index in range(3)]
    for copy in pack(sizes, half[0], *indices, ocean, weight, out, staged, out_sems):
        copy.wait()


def edge_lane(takes, width, high):
    def lane(line):
        at, first = jnp.full(line.shape, -1, jnp.int32), 0
        for index, take in enumerate(takes):
            inside = (line >= first) & (line < first + take)
            start = index * width + (width - take if high else 0)
            at = jnp.where(inside, start + line - first, at)
            first += take
        return at

    return lane


def strip_lane(first, chans, width):
    def lane(line):
        at, place = jnp.full(line.shape, -1, jnp.int32), line % STRIP
        start = (first + line // STRIP) * width
        low = (place >= ITERS) & (place < 3 * ITERS)
        high = (place >= 3 * ITERS) & (place < 5 * ITERS)
        at = jnp.where(low, start + place - ITERS, at)
        at = jnp.where(high, start + width + place - 5 * ITERS, at)
        return jnp.where(line < chans * STRIP, at, -1)

    return lane


def fill_strip(own, left, right, first, chans, take):
    pieces = []
    gap = [jnp.zeros((ITERS - take, own.shape[1]), F32)] if take < ITERS else []
    for chan in range(chans):
        beside = slice(first + chan * take, first + (chan + 1) * take)
        inner = slice(chan * STRIP + ITERS, (chan + 1) * STRIP - ITERS)
        pieces += gap + [left[beside, :], own[inner, :], right[beside, :]] + gap
    pieces.append(jnp.zeros((own.shape[0] - chans * STRIP, own.shape[1]), F32))
    return jnp.concatenate(pieces, axis=0)


def edge_columns(pieces, outputs):
    width = pieces[0][0].shape[1]
    length = outputs[0][0].shape[1]
    tail = length - sum(piece.shape[0] for piece in pieces[0])
    whole = jnp.concatenate(
        [jnp.concatenate([*piece, jnp.zeros((tail, width), F32)], axis=0) for piece in pieces],
        axis=1,
    )
    rows = []
    for ref, lane in outputs:
        shape = (ref.shape[0], whole.shape[1])
        rows.append(iota(shape, 1) == lane(iota(shape, 0)))
    select = one_hot(jnp.concatenate([row.astype(jnp.int32) for row in rows], axis=0) > 0)
    top, middle, bottom = split3(whole)
    edges = dot(select, bottom, (1, 1)) + dot(select, middle, (1, 1))
    edges = edges + dot(select, top, (1, 1))
    first = 0
    for ref, _ in outputs:
        ref[...] = edges[first : first + ref.shape[0]]
        first += ref.shape[0]


def first_columns_kernel(before, after, atm, diff, low, high, own):
    chans, _, width = atm.target.shape
    bodies = [ref.get()[chan] for ref in (atm, diff) for chan in range(chans)]
    takes = [1] * chans + [ITERS - 1] * chans
    pieces = [(before[i], body, after[i]) for i, body in enumerate(bodies)]
    edge_columns(
        pieces,
        [
            (low, edge_lane(takes, width, False)),
            (high, edge_lane(takes, width, True)),
            (own, strip_lane(chans, chans, width)),
        ],
    )


def columns_kernel(before, body, after, low, high, own):
    chans, _, width = body.shape
    pieces = [(before[i], body[i], after[i]) for i in range(chans)]
    edge_columns(
        pieces,
        [
            (low, edge_lane([ITERS] * chans, width, False)),
            (high, edge_lane([ITERS] * chans, width, True)),
            (own, strip_lane(0, chans, width)),
        ],
    )


def beside_rows(x):
    rows = x.shape[0]
    return pltpu.roll(x, rows - 1, 0) + pltpu.roll(x, 1, 0)


def beside_columns(x):
    width = x.shape[1]
    return pltpu.roll(x, width - 1, 1), pltpu.roll(x, 1, 1)


def beside_body(body, side=None):
    rows, width = body.shape
    lane = iota(body.shape, 1)
    east, west = beside_columns(body)
    east = jnp.where(lane == width - 1, 0.0 if side is None else side, east)
    west = jnp.where(lane == 0, 0.0 if side is None else side, west)
    return beside_rows(body) + east + west


def smooth_kernel(cap, before, after, left, right, atm, dest, seg, table, seg_select, held, sems):
    chans, rows, width = atm.target.shape
    segs, slots = held.shape
    target = dest.get()[...]
    slot = target * cap + positions(target, slots // cap)
    place = one_hot(iota((slots, target.shape[1]), 0) == slot)
    member = one_hot(iota((segs, target.shape[1]), 0) == seg.get()[...])
    held[...] = dot(member, place, (1, 1)).astype(BF16)
    stores = [pltpu.make_async_copy(held, seg_select, sems.at[0])]
    stores[0].start()
    sides = nearest_columns(left, right, width, chans)
    state = atm.get()
    parts = []
    for chan in range(chans):
        body = jnp.concatenate([before[chan], state[chan], after[chan]], axis=0)
        side = sides[: body.shape[0], chan * width : (chan + 1) * width]
        parts.append(split3((0.5 * body + 0.125 * beside_body(body, side))[EDGE : EDGE + rows]))
    table[...] = jnp.concatenate([p[level] for level in (2, 1, 0) for p in parts], axis=1)
    for store in stores:
        store.wait()


def nearest_columns(left, right, width, chans):
    edges = jnp.concatenate([left[:EDGE, :], right[:EDGE, :]], axis=0)
    shape = (6 * EDGE, chans * width)
    which, lane = iota(shape, 0), iota(shape, 1)
    line = which % (2 * EDGE)
    at = jnp.where(line < EDGE, line * width, (line - EDGE) * width + width - 1)
    select = one_hot((lane == at) & (line % EDGE < chans))
    return dot(jnp.concatenate(split3(edges), axis=0), select, (0, 0))


def flux_kernel(cap, ocn_count, mirrored, half, incoming, table, *rest):
    out, label_rows, staged, sems = rest[-4:]
    incoming = incoming if mirrored else incoming.get()
    owners, _, width = incoming.shape
    chans = staged.shape[1] // cap
    rows = table.shape[0]
    across = ocn_count // 2
    base = (1 - half[0] if mirrored else half[0]) * across
    groups = 2
    each = owners // groups
    stores = []
    label_rows[...] = incoming[:, (chans + 1) * cap, :]
    for group in range(groups):
        part_of = slice(group * each, (group + 1) * each)

        def part(index):
            piece = incoming[part_of, index * cap : (index + 1) * cap, :]
            return piece.reshape(each * cap, width)

        labels = incoming[part_of, (chans + 1) * cap :, :]
        labels = jnp.concatenate(
            [labels[i, :, j : j + 1] for i in range(each) for j in range(cap // EDGE)], axis=0
        ).astype(jnp.int32)
        select = one_hot(iota((each * cap, rows), 1) == labels)
        found = dot(select, table[...])
        pieces = [found[:, i * width : (i + 1) * width] for i in range(3 * chans)]
        air = [(pieces[i] + pieces[chans + i]) + pieces[2 * chans + i] for i in range(chans)]
        wind_east = air[1] - part(1)
        wind_north = air[2] - part(2)
        wind_speed = jnp.sqrt(wind_east * wind_east + wind_north * wind_north + 0.5)
        temp_gap = part(0) - air[0]
        factor = 1.0 + 0.5 * jnp.tanh(temp_gap / wind_speed)
        common = part(3) * factor * wind_speed
        for index, value in enumerate((0.8 * temp_gap, 0.6 * wind_east, 0.6 * wind_north)):
            staged[part_of, index * cap : (index + 1) * cap, :] = (common * value).reshape(
                each, cap, width
            )
        for line in range(group * each // across, (group + 1) * each // across):
            store = pltpu.make_async_copy(
                staged.at[pl.ds(line * across, across)],
                out.at[pl.ds(line * ocn_count + base, across)],
                sems.at[line],
            )
            store.start()
            stores.append(store)
    for store in stores:
        store.wait()


def forced_kernel(
    cap, ocn_count, half, own_labels, mirror_labels, weighted, atm, forced, top, bottom, held, sems
):
    owners, width = own_labels.shape
    devices = 2 * owners
    chans, rows, _ = forced.shape
    slots = devices * cap
    log = cap.bit_length() - 1
    across = ocn_count // 2
    loads = [
        pltpu.make_async_copy(
            weighted.at[pl.ds(line * ocn_count + base * across, across)],
            held.at[pl.ds(side * owners + line * across, across)],
            sems.at[side * (owners // across) + line],
        )
        for side, base in enumerate((half[0], 1 - half[0]))
        for line in range(owners // across)
    ]
    for load in loads:
        load.start()
    labels = jnp.concatenate([own_labels[...], mirror_labels[...]], axis=0).astype(jnp.int32)
    spread = one_hot(iota((width, slots), 0) == (iota((width, slots), 1) & (cap - 1)) + FLAT)
    coarse = dot(lax.shift_right_logical(labels, 5).astype(F32).astype(BF16), spread)
    fine = dot((labels & 31).astype(F32).astype(BF16), spread)
    owner = lax.shift_right_logical(iota((devices, slots), 1), log)
    label = jnp.where(owner == iota((devices, slots), 0), coarse * 32.0 + fine, 0.0)
    label = jnp.sum(label, axis=0, keepdims=True).astype(jnp.int32)
    select = one_hot(iota((rows, slots), 0) == label)
    state = atm.get()
    for load in loads:
        load.wait()
    values = [
        held[:, chan * cap : (chan + 1) * cap, :].reshape(slots, width) for chan in range(chans)
    ]
    for chan, air_sum in enumerate(exact_dots(select, values)):
        result = state[chan] + air_sum if chan == 0 else state[chan] - air_sum
        forced[chan] = result
        top[chan] = result[:EDGE]
        bottom[chan] = result[-EDGE:]


def diffuse_kernel(
    forced, before, after, diff_own, diff_left, diff_right, diff_before, diff_after, diff,
    out, diff_strip, staged, sems,
):
    chans, rows, width = forced.shape
    diff_strip[...] = fill_strip(diff_own, diff_left, diff_right, chans, chans, ITERS - 1)
    stores = []
    for chan in range(chans):
        body = jnp.concatenate([before[chan], forced[chan], after[chan]], axis=0)
        body_diff = [diff_before[chans + chan], diff.get()[chan], diff_after[chans + chan]]
        body_diff = jnp.concatenate(body_diff, axis=0)
        for _ in range(ITERS):
            body = body + body_diff * (beside_body(body) - 4.0 * body)
        staged[chan] = body[EDGE : EDGE + rows]
        stores.append(pltpu.make_async_copy(staged.at[chan], out.at[chan], sems.at[chan]))
        stores[-1].start()
    for store in stores:
        store.wait()


def finish_kernel(
    cap, returned, own, left, right, diff_strip, seg_select, inner, ocean_flux, atm_next,
    flux_staged, staged, sems,
):
    devices, _, width = returned.shape
    chans, rows, _ = staged.shape
    stores = []

    def send(source, target):
        stores.append(pltpu.make_async_copy(source, target, sems.at[len(stores)]))
        stores[-1].start()

    values = [
        returned[:, chan * cap : (chan + 1) * cap, :].reshape(devices * cap, width)
        for chan in range(chans)
    ]
    for chan, total in enumerate(exact_dots(seg_select.get()[...], values)):
        flux_staged[chan] = total
    send(flux_staged, ocean_flux)
    state = fill_strip(own, left, right, 0, chans, ITERS)
    spread = diff_strip[...]
    for _ in range(ITERS):
        east, west = beside_columns(state)
        state = state + spread * ((beside_rows(state) + east + west) - 4.0 * state)
    lines = state.shape[0]
    shape = (3 * lines, chans * width)
    which, lane = iota(shape, 0) % lines, iota(shape, 1)
    place, start = which % STRIP, which // STRIP * width
    low = (place >= ITERS) & (place < 2 * ITERS) & (lane == start + place - ITERS)
    high = (place >= 4 * ITERS) & (place < 5 * ITERS)
    high = high & (lane == start + width + place - 5 * ITERS)
    select = one_hot((which < chans * STRIP) & (low | high))
    edges = dot(jnp.concatenate(split3(state), axis=0), select, (0, 0))
    lane = iota((rows, width), 1)
    outer = (lane < ITERS) | (lane >= width - ITERS)
    middle = inner.get()
    for chan in range(chans):
        edge = edges[EDGE : EDGE + rows, chan * width : (chan + 1) * width]
        staged[chan] = jnp.where(outer, edge, middle[chan])
        send(staged.at[chan], atm_next.at[chan])
    for store in stores:
        store.wait()


def shift(axis, low_edge, high_edge):
    count = lax.axis_size(axis)
    forward = [(i, i + 1) for i in range(count - 1)]
    backward = [(target, source) for source, target in forward]
    return lax.ppermute(high_edge, axis, forward), lax.ppermute(low_edge, axis, backward)


def per_device(atm, diff, ocean, mask, area, seg, dest, row):
    atm_count, ocn_count = lax.axis_size("atm"), lax.axis_size("ocn")
    devices = atm_count * ocn_count
    rows, chans, width = atm.shape
    count = seg.shape[0]
    segs = ocean.shape[0]
    cap = max(2, 2 * count // devices)
    slots = devices * cap
    atm = jnp.transpose(atm, (1, 0, 2))
    diff = jnp.transpose(diff, (1, 0, 2))
    ocean = jnp.transpose(ocean, (1, 0, 2))

    def shape(*dims, dtype=F32):
        return jax.ShapeDtypeStruct(dims, dtype)

    hbm, fast = pltpu.HBM, pl.BlockSpec(memory_space=pltpu.VMEM)
    slow = pl.BlockSpec(memory_space=hbm)
    dest, seg, row = dest.reshape(1, count), seg.reshape(1, count), row.reshape(1, count)
    across = ocn_count // 2
    owners = devices // 2
    half = (lax.axis_index("ocn") // across).astype(jnp.int32).reshape(1)
    halves = [
        [i * ocn_count + side * across + j for i in range(atm_count) for j in range(across)]
        for side in range(2)
    ]
    mirror = [(j, (j + across) % ocn_count) for j in range(ocn_count)]
    sizes = (devices, ocn_count, cap)
    packed = (owners, (chans + 1) * cap + EDGE, width)
    lines_sent = chans * segs + count + -(-3 * count // width // 16) * 16

    def exchange(x):
        return lax.all_to_all(
            x, BOTH, split_axis=0, concat_axis=0, tiled=True, axis_index_groups=halves
        )

    sent = call(
        send_kernel,
        hbm((lines_sent, width), F32),
        (ocean, seg, mask, area, dest, row),
        late=(0, 1, 2, 3, 4, 5),
        outs=slow,
        scratch=[
            pltpu.VMEM((lines_sent - chans * segs, width), F32),
            pltpu.SemaphoreType.DMA((chans + 1,)),
        ],
        cost=COST_SEND,
    )
    received = lax.ppermute(sent, "ocn", mirror)

    def packing(sent, late, cost, *ahead):
        return call(
            functools.partial(pack_kernel, sizes, count, chans),
            hbm(packed, F32),
            (half, sent),
            smem=(0,),
            late=late,
            after=ahead,
            outs=slow,
            scratch=[pltpu.VMEM(packed, F32), pltpu.SemaphoreType.DMA((chans + 2,))],
            cost=cost,
        )

    first = jnp.concatenate([atm[:, :EDGE], diff[:, :EDGE]], axis=0)
    final = jnp.concatenate([atm[:, -EDGE:], diff[:, -EDGE:]], axis=0)
    before, after = shift("atm", first, final)
    own_packed = packing(sent, (1,), COST_OWN)
    own_incoming = exchange(own_packed)
    long = -(-(rows + 2 * EDGE) // 128) * 128

    def lines(columns):
        return shape(-(-columns // EDGE) * EDGE, long)

    low, high, diff_own = call(
        first_columns_kernel,
        (lines(chans * ITERS), lines(chans * ITERS), lines(chans * STRIP)),
        (before, after, atm, diff),
        late=(2, 3),
        after=(own_packed,),
        cost=COST_FIRST,
    )
    left, right = shift("ocn", low, high)
    mirror_packed = packing(received, (), COST_MIRROR, diff_own)
    mirror_incoming = exchange(mirror_packed)

    table, seg_select = call(
        functools.partial(smooth_kernel, cap),
        (pltpu.VMEM((rows, 3 * chans * width), BF16), hbm((segs, slots), BF16)),
        (before, after, left, right, atm, dest, seg),
        late=(4, 5, 6),
        after=(mirror_packed,),
        outs=(fast, slow),
        cost=COST_SMOOTH,
        scratch=[pltpu.VMEM((segs, slots), BF16), pltpu.SemaphoreType.DMA((1,))],
    )

    def flux(incoming, mirrored, begun):
        return call(
            functools.partial(flux_kernel, cap, ocn_count, mirrored),
            (
                hbm((devices, chans * cap, width), F32),
                shape(owners, width),
            ),
            (half, incoming, table, *begun),
            smem=(0,),
            late=() if mirrored else (1,),
            outs=(slow, fast),
            scratch=[
                pltpu.VMEM((owners, chans * cap, width), F32),
                pltpu.SemaphoreType.DMA((atm_count,)),
            ],
            aliases={3: 0} if begun else {},
        )

    begun, own_labels = flux(own_incoming, False, ())
    weighted, mirror_labels = flux(mirror_incoming, True, (begun,))
    returned = lax.all_to_all(weighted, BOTH, split_axis=0, concat_axis=0, tiled=True)
    forced, top, bottom = call(
        functools.partial(forced_kernel, cap, ocn_count),
        (
            pltpu.VMEM((chans, rows, width), F32),
            shape(chans, EDGE, width),
            shape(chans, EDGE, width),
        ),
        (half, own_labels, mirror_labels, weighted, atm),
        smem=(0,),
        plain=(3,),
        late=(4,),
        scratch=[
            pltpu.VMEM((devices, chans * cap, width), F32),
            pltpu.SemaphoreType.DMA((2 * atm_count,)),
        ],
    )
    forced_before, forced_after = shift("atm", top, bottom)
    forced_low, forced_high, forced_own = call(
        columns_kernel,
        (lines(chans * ITERS), lines(chans * ITERS), lines(chans * STRIP)),
        (forced_before, forced, forced_after),
    )
    forced_left, forced_right = shift("ocn", forced_low, forced_high)
    inner, diff_strip = call(
        diffuse_kernel,
        (hbm((chans, rows, width), F32), lines(chans * STRIP)),
        (forced, forced_before, forced_after, diff_own, left, right, before, after, diff),
        late=(8,),
        outs=(slow, fast),
        scratch=[pltpu.VMEM((chans, rows, width), F32), pltpu.SemaphoreType.DMA((chans,))],
    )
    ocean_flux, atm_next = call(
        functools.partial(finish_kernel, cap),
        (hbm((chans, segs, width), F32), hbm((chans, rows, width), F32)),
        (returned, forced_own, forced_left, forced_right, diff_strip, seg_select, inner),
        late=(5, 6),
        outs=(slow, slow),
        scratch=[
            pltpu.VMEM((chans, segs, width), F32),
            pltpu.VMEM((chans, rows, width), F32),
            pltpu.SemaphoreType.DMA((1 + chans,)),
        ],
    )
    return jnp.transpose(atm_next, (1, 0, 2)), jnp.transpose(ocean_flux, (1, 0, 2))


def solution(mesh):
    placed = (
        P("atm", None, "ocn"),
        P("atm", None, "ocn"),
        P(BOTH, None, None),
        P(BOTH, None),
        P(BOTH, None),
        P(BOTH),
        P(BOTH, None),
        P(BOTH),
    )
    return jax.shard_map(
        per_device,
        mesh=mesh,
        in_specs=placed,
        out_specs=(P("atm", None, "ocn"), P(BOTH, None, None)),
        check_vma=False,
    )
```

```python
import functools

import jax
import jax.numpy as jnp
from jax import lax
from jax.experimental import pallas as pl
from jax.experimental.pallas import tpu as pltpu
from jax.sharding import PartitionSpec as P

ITERS = 3
EDGE = 8
FLAT = 32
STRIP = 6 * ITERS
COST_SEND = 1 << 10
COST_OWN = 1 << 10
COST_MIRROR = 16 << 20
COST_FIRST = 1 << 10
COST_SMOOTH = 100 << 20
BOTH = ("atm", "ocn")
F32 = jnp.float32
BF16 = jnp.bfloat16


def split3(x):
    high = x.astype(BF16)
    rest = x - high.astype(F32)
    middle = rest.astype(BF16)
    low = (rest - middle.astype(F32)).astype(BF16)
    return high, middle, low


def dot(a, b, contract=(1, 0)):
    dims = (((contract[0],), (contract[1],)), ((), ()))
    return lax.dot_general(a, b, dims, preferred_element_type=F32)


def exact_dots(select, values, contract=(1, 0)):
    parts = [split3(x) for x in values]
    stacked = jnp.concatenate([p[level] for level in (2, 1, 0) for p in parts], axis=1)
    width, count = values[0].shape[1], len(values)
    result = dot(select, stacked, contract)

    def piece(level, index):
        at = (level * count + index) * width
        return result[:, at : at + width]

    return [(piece(0, i) + piece(1, i)) + piece(2, i) for i in range(count)]


def iota(shape, dim):
    return lax.broadcasted_iota(jnp.int32, shape, dim)


def one_hot(condition):
    return condition.astype(F32).astype(BF16)


class Late:
    def __init__(self, source, target, sem):
        self.target, self.copy = target, pltpu.make_async_copy(source, target, sem)
        self.copy.start()

    def get(self):
        if self.copy is not None:
            self.copy.wait()
            self.copy = None
        return self.target


def call(
    kernel, out_shape, operands, *, late=(), plain=(), smem=(), after=(), outs=None, cost=None, scratch=(), aliases={},
):
    total = sum(x.size * x.dtype.itemsize for x in operands)
    extra = {} if outs is None else {"out_specs": outs}
    count = len(operands)
    operands = [*operands, *after]
    unread = range(count, len(operands))
    slow = [*late, *plain, *aliases]
    given = [
        pltpu.with_memory_space_constraint(x, pltpu.HBM) if i in slow else x
        for i, x in enumerate(operands)
    ]
    results = len(jax.tree.leaves(out_shape))

    def body(*refs):
        first, second = len(operands), len(operands) + results
        inputs, held = list(refs[:count]), refs[second : second + len(late)]
        rest = refs[second + len(late) :]
        if late:
            sems, rest = rest[0], rest[1:]
            for at, i in enumerate(late):
                inputs[i] = Late(inputs[i], held[at], sems.at[at])
        kernel(*inputs, *refs[first:second], *rest)

    held = [pltpu.VMEM(operands[i].shape, operands[i].dtype) for i in late]
    held += [pltpu.SemaphoreType.DMA((len(late),))] if late else []

    def space(i):
        if i in unread:
            return pl.ANY
        return pltpu.HBM if i in slow else pltpu.SMEM if i in smem else pltpu.VMEM

    return pl.pallas_call(
        body,
        out_shape=out_shape,
        in_specs=[pl.BlockSpec(memory_space=space(i)) for i in range(len(operands))],
        scratch_shapes=held + list(scratch),
        input_output_aliases=aliases,
        compiler_params=pltpu.CompilerParams(vmem_limit_bytes=16 << 20),
        cost_estimate=pl.CostEstimate(flops=(cost or 0) * 1000, bytes_accessed=cost or total, transcendentals=0),
        **extra,
    )(*given)


def positions(target, devices):
    count = target.shape[1]
    earlier = one_hot(iota((count, count), 0) < iota((count, count), 1))
    match = iota((devices, count), 0) == target
    before = dot(one_hot(match), earlier)
    return jnp.sum(jnp.where(match, before, 0.0), axis=0, keepdims=True).astype(jnp.int32)


def pack(sizes, half, target, seg, value, ocean, weight, out, staged, out_sems):
    devices, ocn_count, cap = sizes
    across = ocn_count // 2
    owners = devices // 2
    slots = owners * cap
    count = target.shape[1]
    chans, (segs, width) = len(ocean), ocean[0].shape
    stores = []

    def send(index, size, values):
        piece = pl.ds(index * cap, size)
        staged[:, piece, :] = values.reshape(owners, size, width)
        store = pltpu.make_async_copy(
            staged.at[:, piece, :], out.at[:, piece, :], out_sems.at[index]
        )
        store.start()
        stores.append(store)

    position = positions(target, devices)
    beside = target % ocn_count
    group = target // ocn_count * across + beside % across
    group = jnp.where(beside // across == half, group, owners)
    slot = group * cap + position
    place = one_hot(iota((slots, count), 0) == slot)
    member = one_hot(iota((segs, count), 0) == seg)
    of_seg = dot(place, member, (1, 1)).astype(BF16)
    for chan, sent in enumerate(exact_dots(of_seg, ocean)):
        send(chan, cap, sent)
    (reach,) = exact_dots(place, [weight])
    send(chans, cap, reach)
    line = iota((owners * EDGE, count), 0)
    tall = line == group * EDGE + (position & (EDGE - 1))
    flat = line == group * EDGE
    lane = iota((width, count), 0)
    tall_lane = lane == lax.shift_right_logical(position, EDGE.bit_length() - 1)
    flat_lane = lane == position + FLAT
    coarse, fine = lax.shift_right_logical(value, 5).astype(F32), (value & 31).astype(F32)
    lanes = jnp.concatenate(
        [
            jnp.concatenate([jnp.where(at, v, 0.0) for at in (tall_lane, flat_lane)], axis=1)
            for v in (coarse, fine)
        ],
        axis=0,
    ).astype(BF16)
    labels = dot(jnp.concatenate([one_hot(tall), one_hot(flat)], axis=1), lanes, (1, 1))
    send(chans + 1, EDGE, labels[:, :width] * 32.0 + labels[:, width:])
    return stores


def send_kernel(seg, mask, area, dest, row, ocean, sent):
    segs, width = mask.target.shape
    count = area.target.shape[0]
    lines = count // width
    chans = ocean.target.shape[0]
    first = chans * segs
    found = seg.get()[...]
    member = one_hot(iota((segs, count), 0) == found)
    sea = dot(member, mask.get()[...].astype(F32).astype(BF16), (0, 0))
    sent[first : first + count, :] = area.get()[...] * sea
    flat = [
        index[:, line * width : (line + 1) * width].astype(F32)
        for index in (dest.get()[...], found, row.get()[...])
        for line in range(lines)
    ]
    rest = sent.shape[0] - first - count - len(flat)
    sent[first + count :, :] = jnp.concatenate(flat + [jnp.zeros((rest, width), F32)], axis=0)
    values = ocean.get()
    for chan in range(chans):
        sent[chan * segs : (chan + 1) * segs, :] = values[chan]


def pack_kernel(sizes, count, chans, half, sent, out, staged, out_sems):
    width = sent.shape[1]
    lines = count // width
    rest = -(-3 * lines // 16) * 16
    segs = (sent.shape[0] - count - rest) // chans
    first = chans * segs + count

    def vector(index):
        at = first + index * lines
        pieces = [sent[at + line : at + line + 1, :] for line in range(lines)]
        return jnp.concatenate(pieces, axis=1).astype(jnp.int32)

    ocean = [sent[chan * segs : (chan + 1) * segs, :] for chan in range(chans)]
    weight = sent[chans * segs : first, :]
    indices = [vector(index) for index in range(3)]
    for copy in pack(sizes, half[0], *indices, ocean, weight, out, staged, out_sems):
        copy.wait()


def edge_lane(takes, width, high):
    def lane(line):
        at, first = jnp.full(line.shape, -1, jnp.int32), 0
        for index, take in enumerate(takes):
            inside = (line >= first) & (line < first + take)
            start = index * width + (width - take if high else 0)
            at = jnp.where(inside, start + line - first, at)
            first += take
        return at

    return lane


def strip_lane(first, chans, width):
    def lane(line):
        at, place = jnp.full(line.shape, -1, jnp.int32), line % STRIP
        start = (first + line // STRIP) * width
        low = (place >= ITERS) & (place < 3 * ITERS)
        high = (place >= 3 * ITERS) & (place < 5 * ITERS)
        at = jnp.where(low, start + place - ITERS, at)
        at = jnp.where(high, start + width + place - 5 * ITERS, at)
        return jnp.where(line < chans * STRIP, at, -1)

    return lane


def fill_strip(own, left, right, first, chans, take):
    pieces = []
    gap = [jnp.zeros((ITERS - take, own.shape[1]), F32)] if take < ITERS else []
    for chan in range(chans):
        beside = slice(first + chan * take, first + (chan + 1) * take)
        inner = slice(chan * STRIP + ITERS, (chan + 1) * STRIP - ITERS)
        pieces += gap + [left[beside, :], own[inner, :], right[beside, :]] + gap
    pieces.append(jnp.zeros((own.shape[0] - chans * STRIP, own.shape[1]), F32))
    return jnp.concatenate(pieces, axis=0)


def edge_columns(pieces, outputs):
    width = pieces[0][0].shape[1]
    length = outputs[0][0].shape[1]
    tail = length - sum(piece.shape[0] for piece in pieces[0])
    whole = jnp.concatenate(
        [jnp.concatenate([*piece, jnp.zeros((tail, width), F32)], axis=0) for piece in pieces],
        axis=1,
    )
    rows = []
    for ref, lane in outputs:
        shape = (ref.shape[0], whole.shape[1])
        rows.append(iota(shape, 1) == lane(iota(shape, 0)))
    select = one_hot(jnp.concatenate([row.astype(jnp.int32) for row in rows], axis=0) > 0)
    top, middle, bottom = split3(whole)
    edges = dot(select, bottom, (1, 1)) + dot(select, middle, (1, 1))
    edges = edges + dot(select, top, (1, 1))
    first = 0
    for ref, _ in outputs:
        ref[...] = edges[first : first + ref.shape[0]]
        first += ref.shape[0]


def first_columns_kernel(before, after, atm, diff, low, high, own):
    chans, _, width = atm.target.shape
    bodies = [ref.get()[chan] for ref in (atm, diff) for chan in range(chans)]
    takes = [1] * chans + [ITERS - 1] * chans
    pieces = [(before[i], body, after[i]) for i, body in enumerate(bodies)]
    edge_columns(
        pieces,
        [
            (low, edge_lane(takes, width, False)),
            (high, edge_lane(takes, width, True)),
            (own, strip_lane(chans, chans, width)),
        ],
    )


def columns_kernel(before, body, after, low, high, own):
    chans, _, width = body.shape
    pieces = [(before[i], body[i], after[i]) for i in range(chans)]
    edge_columns(
        pieces,
        [
            (low, edge_lane([ITERS] * chans, width, False)),
            (high, edge_lane([ITERS] * chans, width, True)),
            (own, strip_lane(0, chans, width)),
        ],
    )


def beside_rows(x):
    rows = x.shape[0]
    return pltpu.roll(x, rows - 1, 0) + pltpu.roll(x, 1, 0)


def beside_columns(x):
    width = x.shape[1]
    return pltpu.roll(x, width - 1, 1), pltpu.roll(x, 1, 1)


def beside_body(body, side=None):
    rows, width = body.shape
    lane = iota(body.shape, 1)
    east, west = beside_columns(body)
    east = jnp.where(lane == width - 1, 0.0 if side is None else side, east)
    west = jnp.where(lane == 0, 0.0 if side is None else side, west)
    return beside_rows(body) + east + west


def smooth_kernel(cap, before, after, left, right, atm, dest, seg, table, seg_select, held, sems):
    chans, rows, width = atm.target.shape
    segs, slots = held.shape
    target = dest.get()[...]
    slot = target * cap + positions(target, slots // cap)
    place = one_hot(iota((slots, target.shape[1]), 0) == slot)
    member = one_hot(iota((segs, target.shape[1]), 0) == seg.get()[...])
    held[...] = dot(member, place, (1, 1)).astype(BF16)
    stores = [pltpu.make_async_copy(held, seg_select, sems.at[0])]
    stores[0].start()
    sides = nearest_columns(left, right, width, chans)
    state = atm.get()
    parts = []
    for chan in range(chans):
        body = jnp.concatenate([before[chan], state[chan], after[chan]], axis=0)
        side = sides[: body.shape[0], chan * width : (chan + 1) * width]
        parts.append(split3((0.5 * body + 0.125 * beside_body(body, side))[EDGE : EDGE + rows]))
    table[...] = jnp.concatenate([p[level] for level in (2, 1, 0) for p in parts], axis=1)
    for store in stores:
        store.wait()


def nearest_columns(left, right, width, chans):
    edges = jnp.concatenate([left[:EDGE, :], right[:EDGE, :]], axis=0)
    shape = (6 * EDGE, chans * width)
    which, lane = iota(shape, 0), iota(shape, 1)
    line = which % (2 * EDGE)
    at = jnp.where(line < EDGE, line * width, (line - EDGE) * width + width - 1)
    select = one_hot((lane == at) & (line % EDGE < chans))
    return dot(jnp.concatenate(split3(edges), axis=0), select, (0, 0))


def flux_kernel(cap, ocn_count, mirrored, half, incoming, table, *rest):
    out, label_rows, staged, sems = rest[-4:]
    incoming = incoming if mirrored else incoming.get()
    owners, _, width = incoming.shape
    chans = staged.shape[1] // cap
    rows = table.shape[0]
    across = ocn_count // 2
    base = (1 - half[0] if mirrored else half[0]) * across
    groups = 2
    each = owners // groups
    stores = []
    label_rows[...] = incoming[:, (chans + 1) * cap, :]
    for group in range(groups):
        part_of = slice(group * each, (group + 1) * each)

        def part(index):
            piece = incoming[part_of, index * cap : (index + 1) * cap, :]
            return piece.reshape(each * cap, width)

        labels = incoming[part_of, (chans + 1) * cap :, :]
        labels = jnp.concatenate(
            [labels[i, :, j : j + 1] for i in range(each) for j in range(cap // EDGE)], axis=0
        ).astype(jnp.int32)
        select = one_hot(iota((each * cap, rows), 1) == labels)
        found = dot(select, table[...])
        pieces = [found[:, i * width : (i + 1) * width] for i in range(3 * chans)]
        air = [(pieces[i] + pieces[chans + i]) + pieces[2 * chans + i] for i in range(chans)]
        wind_east = air[1] - part(1)
        wind_north = air[2] - part(2)
        wind_speed = jnp.sqrt(wind_east * wind_east + wind_north * wind_north + 0.5)
        temp_gap = part(0) - air[0]
        factor = 1.0 + 0.5 * jnp.tanh(temp_gap / wind_speed)
        common = part(3) * factor * wind_speed
        for index, value in enumerate((0.8 * temp_gap, 0.6 * wind_east, 0.6 * wind_north)):
            staged[part_of, index * cap : (index + 1) * cap, :] = (common * value).reshape(
                each, cap, width
            )
        for line in range(group * each // across, (group + 1) * each // across):
            store = pltpu.make_async_copy(
                staged.at[pl.ds(line * across, across)],
                out.at[pl.ds(line * ocn_count + base, across)],
                sems.at[line],
            )
            store.start()
            stores.append(store)
    for store in stores:
        store.wait()


def forced_kernel(
    cap, ocn_count, half, own_labels, mirror_labels, weighted, atm, forced, top, bottom, held, sems
):
    owners, width = own_labels.shape
    devices = 2 * owners
    chans, rows, _ = forced.shape
    slots = devices * cap
    log = cap.bit_length() - 1
    across = ocn_count // 2
    loads = [
        pltpu.make_async_copy(
            weighted.at[pl.ds(line * ocn_count + base * across, across)],
            held.at[pl.ds(side * owners + line * across, across)],
            sems.at[side * (owners // across) + line],
        )
        for side, base in enumerate((half[0], 1 - half[0]))
        for line in range(owners // across)
    ]
    for load in loads:
        load.start()
    labels = jnp.concatenate([own_labels[...], mirror_labels[...]], axis=0).astype(jnp.int32)
    spread = one_hot(iota((width, slots), 0) == (iota((width, slots), 1) & (cap - 1)) + FLAT)
    coarse = dot(lax.shift_right_logical(labels, 5).astype(F32).astype(BF16), spread)
    fine = dot((labels & 31).astype(F32).astype(BF16), spread)
    owner = lax.shift_right_logical(iota((devices, slots), 1), log)
    label = jnp.where(owner == iota((devices, slots), 0), coarse * 32.0 + fine, 0.0)
    label = jnp.sum(label, axis=0, keepdims=True).astype(jnp.int32)
    select = one_hot(iota((rows, slots), 0) == label)
    state = atm.get()
    for load in loads:
        load.wait()
    values = [
        held[:, chan * cap : (chan + 1) * cap, :].reshape(slots, width) for chan in range(chans)
    ]
    for chan, air_sum in enumerate(exact_dots(select, values)):
        result = state[chan] + air_sum if chan == 0 else state[chan] - air_sum
        forced[chan] = result
        top[chan] = result[:EDGE]
        bottom[chan] = result[-EDGE:]


def diffuse_kernel(
    forced, before, after, diff_own, diff_left, diff_right, diff_before, diff_after, diff,
    out, diff_strip, staged, sems,
):
    chans, rows, width = forced.shape
    diff_strip[...] = fill_strip(diff_own, diff_left, diff_right, chans, chans, ITERS - 1)
    stores = []
    for chan in range(chans):
        body = jnp.concatenate([before[chan], forced[chan], after[chan]], axis=0)
        body_diff = [diff_before[chans + chan], diff.get()[chan], diff_after[chans + chan]]
        body_diff = jnp.concatenate(body_diff, axis=0)
        for _ in range(ITERS):
            body = body + body_diff * (beside_body(body) - 4.0 * body)
        staged[chan] = body[EDGE : EDGE + rows]
        stores.append(pltpu.make_async_copy(staged.at[chan], out.at[chan], sems.at[chan]))
        stores[-1].start()
    for store in stores:
        store.wait()


def finish_kernel(
    cap, returned, own, left, right, diff_strip, seg_select, inner, ocean_flux, atm_next,
    flux_staged, staged, sems,
):
    devices, _, width = returned.shape
    chans, rows, _ = staged.shape
    stores = []

    def send(source, target):
        stores.append(pltpu.make_async_copy(source, target, sems.at[len(stores)]))
        stores[-1].start()

    values = [
        returned[:, chan * cap : (chan + 1) * cap, :].reshape(devices * cap, width)
        for chan in range(chans)
    ]
    for chan, total in enumerate(exact_dots(seg_select.get()[...], values)):
        flux_staged[chan] = total
    send(flux_staged, ocean_flux)
    state = fill_strip(own, left, right, 0, chans, ITERS)
    spread = diff_strip[...]
    for _ in range(ITERS):
        east, west = beside_columns(state)
        state = state + spread * ((beside_rows(state) + east + west) - 4.0 * state)
    lines = state.shape[0]
    shape = (3 * lines, chans * width)
    which, lane = iota(shape, 0) % lines, iota(shape, 1)
    place, start = which % STRIP, which // STRIP * width
    low = (place >= ITERS) & (place < 2 * ITERS) & (lane == start + place - ITERS)
    high = (place >= 4 * ITERS) & (place < 5 * ITERS)
    high = high & (lane == start + width + place - 5 * ITERS)
    select = one_hot((which < chans * STRIP) & (low | high))
    edges = dot(jnp.concatenate(split3(state), axis=0), select, (0, 0))
    lane = iota((rows, width), 1)
    outer = (lane < ITERS) | (lane >= width - ITERS)
    middle = inner.get()
    for chan in range(chans):
        edge = edges[EDGE : EDGE + rows, chan * width : (chan + 1) * width]
        staged[chan] = jnp.where(outer, edge, middle[chan])
        send(staged.at[chan], atm_next.at[chan])
    for store in stores:
        store.wait()


def shift(axis, low_edge, high_edge):
    count = lax.axis_size(axis)
    forward = [(i, i + 1) for i in range(count - 1)]
    backward = [(target, source) for source, target in forward]
    return lax.ppermute(high_edge, axis, forward), lax.ppermute(low_edge, axis, backward)


def per_device(atm, diff, ocean, mask, area, seg, dest, row):
    atm_count, ocn_count = lax.axis_size("atm"), lax.axis_size("ocn")
    devices = atm_count * ocn_count
    rows, chans, width = atm.shape
    count = seg.shape[0]
    segs = ocean.shape[0]
    cap = max(2, 2 * count // devices)
    slots = devices * cap
    atm = jnp.transpose(atm, (1, 0, 2))
    diff = jnp.transpose(diff, (1, 0, 2))
    ocean = jnp.transpose(ocean, (1, 0, 2))

    def shape(*dims, dtype=F32):
        return jax.ShapeDtypeStruct(dims, dtype)

    hbm, fast = pltpu.HBM, pl.BlockSpec(memory_space=pltpu.VMEM)
    slow = pl.BlockSpec(memory_space=hbm)
    dest, seg, row = dest.reshape(1, count), seg.reshape(1, count), row.reshape(1, count)
    across = ocn_count // 2
    owners = devices // 2
    half = (lax.axis_index("ocn") // across).astype(jnp.int32).reshape(1)
    halves = [
        [i * ocn_count + side * across + j for i in range(atm_count) for j in range(across)]
        for side in range(2)
    ]
    mirror = [(j, (j + across) % ocn_count) for j in range(ocn_count)]
    sizes = (devices, ocn_count, cap)
    packed = (owners, (chans + 1) * cap + EDGE, width)
    lines_sent = chans * segs + count + -(-3 * count // width // 16) * 16

    def exchange(x):
        return lax.all_to_all(
            x, BOTH, split_axis=0, concat_axis=0, tiled=True, axis_index_groups=halves
        )

    sent = call(
        send_kernel,
        shape(lines_sent, width),
        (seg, mask, area, dest, row, ocean),
        late=(0, 1, 2, 3, 4, 5),
        cost=COST_SEND,
    )
    received = lax.ppermute(sent, "ocn", mirror)

    def packing(sent, cost, *ahead):
        return call(
            functools.partial(pack_kernel, sizes, count, chans),
            hbm(packed, F32),
            (half, sent),
            smem=(0,),
            after=ahead,
            outs=slow,
            scratch=[pltpu.VMEM(packed, F32), pltpu.SemaphoreType.DMA((chans + 2,))],
            cost=cost,
        )

    first = jnp.concatenate([atm[:, :EDGE], diff[:, :EDGE]], axis=0)
    final = jnp.concatenate([atm[:, -EDGE:], diff[:, -EDGE:]], axis=0)
    before, after = shift("atm", first, final)
    own_packed = packing(sent, COST_OWN)
    own_incoming = exchange(own_packed)
    long = -(-(rows + 2 * EDGE) // 128) * 128

    def lines(columns):
        return shape(-(-columns // EDGE) * EDGE, long)

    low, high, diff_own = call(
        first_columns_kernel,
        (lines(chans * ITERS), lines(chans * ITERS), lines(chans * STRIP)),
        (before, after, atm, diff),
        late=(2, 3),
        after=(own_packed,),
        cost=COST_FIRST,
    )
    left, right = shift("ocn", low, high)
    mirror_packed = packing(received, COST_MIRROR, diff_own)
    mirror_incoming = exchange(mirror_packed)

    table, seg_select = call(
        functools.partial(smooth_kernel, cap),
        (pltpu.VMEM((rows, 3 * chans * width), BF16), hbm((segs, slots), BF16)),
        (before, after, left, right, atm, dest, seg),
        late=(4, 5, 6),
        after=(mirror_packed,),
        outs=(fast, slow),
        cost=COST_SMOOTH,
        scratch=[pltpu.VMEM((segs, slots), BF16), pltpu.SemaphoreType.DMA((1,))],
    )

    def flux(incoming, mirrored, begun):
        return call(
            functools.partial(flux_kernel, cap, ocn_count, mirrored),
            (
                hbm((devices, chans * cap, width), F32),
                shape(owners, width),
            ),
            (half, incoming, table, *begun),
            smem=(0,),
            late=() if mirrored else (1,),
            outs=(slow, fast),
            scratch=[
                pltpu.VMEM((owners, chans * cap, width), F32),
                pltpu.SemaphoreType.DMA((atm_count,)),
            ],
            aliases={3: 0} if begun else {},
        )

    begun, own_labels = flux(own_incoming, False, ())
    weighted, mirror_labels = flux(mirror_incoming, True, (begun,))
    returned = lax.all_to_all(weighted, BOTH, split_axis=0, concat_axis=0, tiled=True)
    forced, top, bottom = call(
        functools.partial(forced_kernel, cap, ocn_count),
        (
            pltpu.VMEM((chans, rows, width), F32),
            shape(chans, EDGE, width),
            shape(chans, EDGE, width),
        ),
        (half, own_labels, mirror_labels, weighted, atm),
        smem=(0,),
        plain=(3,),
        late=(4,),
        scratch=[
            pltpu.VMEM((devices, chans * cap, width), F32),
            pltpu.SemaphoreType.DMA((2 * atm_count,)),
        ],
    )
    forced_before, forced_after = shift("atm", top, bottom)
    forced_low, forced_high, forced_own = call(
        columns_kernel,
        (lines(chans * ITERS), lines(chans * ITERS), lines(chans * STRIP)),
        (forced_before, forced, forced_after),
    )
    forced_left, forced_right = shift("ocn", forced_low, forced_high)
    inner, diff_strip = call(
        diffuse_kernel,
        (hbm((chans, rows, width), F32), lines(chans * STRIP)),
        (forced, forced_before, forced_after, diff_own, left, right, before, after, diff),
        late=(8,),
        outs=(slow, fast),
        scratch=[pltpu.VMEM((chans, rows, width), F32), pltpu.SemaphoreType.DMA((chans,))],
    )
    ocean_flux, atm_next = call(
        functools.partial(finish_kernel, cap),
        (hbm((chans, segs, width), F32), hbm((chans, rows, width), F32)),
        (returned, forced_own, forced_left, forced_right, diff_strip, seg_select, inner),
        late=(5, 6),
        outs=(slow, slow),
        scratch=[
            pltpu.VMEM((chans, segs, width), F32),
            pltpu.VMEM((chans, rows, width), F32),
            pltpu.SemaphoreType.DMA((1 + chans,)),
        ],
    )
    return jnp.transpose(atm_next, (1, 0, 2)), jnp.transpose(ocean_flux, (1, 0, 2))


def solution(mesh):
    placed = (
        P("atm", None, "ocn"),
        P("atm", None, "ocn"),
        P(BOTH, None, None),
        P(BOTH, None),
        P(BOTH, None),
        P(BOTH),
        P(BOTH, None),
        P(BOTH),
    )
    return jax.shard_map(
        per_device,
        mesh=mesh,
        in_specs=placed,
        out_specs=(P("atm", None, "ocn"), P(BOTH, None, None)),
        check_vma=False,
    )
```

```python
import functools

import jax
import jax.numpy as jnp
from jax import lax
from jax.experimental import pallas as pl
from jax.experimental.pallas import tpu as pltpu
from jax.sharding import PartitionSpec as P

ITERS = 3
EDGE = 8
FLAT = 32
STRIP = 6 * ITERS
COST_SEND = 1 << 10
COST_OWN = 1 << 10
COST_MIRROR = 16 << 20
COST_FIRST = 1 << 10
COST_SMOOTH = 100 << 20
BOTH = ("atm", "ocn")
F32 = jnp.float32
BF16 = jnp.bfloat16


def split3(x):
    high = x.astype(BF16)
    rest = x - high.astype(F32)
    middle = rest.astype(BF16)
    low = (rest - middle.astype(F32)).astype(BF16)
    return high, middle, low


def dot(a, b, contract=(1, 0)):
    dims = (((contract[0],), (contract[1],)), ((), ()))
    return lax.dot_general(a, b, dims, preferred_element_type=F32)


def exact_dots(select, values, contract=(1, 0)):
    parts = [split3(x) for x in values]
    stacked = jnp.concatenate([p[level] for level in (2, 1, 0) for p in parts], axis=1)
    width, count = values[0].shape[1], len(values)
    result = dot(select, stacked, contract)

    def piece(level, index):
        at = (level * count + index) * width
        return result[:, at : at + width]

    return [(piece(0, i) + piece(1, i)) + piece(2, i) for i in range(count)]


def iota(shape, dim):
    return lax.broadcasted_iota(jnp.int32, shape, dim)


def one_hot(condition):
    return condition.astype(F32).astype(BF16)


class Late:
    def __init__(self, source, target, sem):
        self.target, self.copy = target, pltpu.make_async_copy(source, target, sem)
        self.copy.start()

    def get(self):
        if self.copy is not None:
            self.copy.wait()
            self.copy = None
        return self.target


def call(
    kernel, out_shape, operands, *, late=(), plain=(), smem=(), after=(), outs=None, cost=None, scratch=(), aliases={},
):
    total = sum(x.size * x.dtype.itemsize for x in operands)
    extra = {} if outs is None else {"out_specs": outs}
    count = len(operands)
    operands = [*operands, *after]
    unread = range(count, len(operands))
    slow = [*late, *plain, *aliases]
    given = [
        pltpu.with_memory_space_constraint(x, pltpu.HBM) if i in slow else x
        for i, x in enumerate(operands)
    ]
    results = len(jax.tree.leaves(out_shape))

    def body(*refs):
        first, second = len(operands), len(operands) + results
        inputs, held = list(refs[:count]), refs[second : second + len(late)]
        rest = refs[second + len(late) :]
        if late:
            sems, rest = rest[0], rest[1:]
            for at, i in enumerate(late):
                inputs[i] = Late(inputs[i], held[at], sems.at[at])
        kernel(*inputs, *refs[first:second], *rest)

    held = [pltpu.VMEM(operands[i].shape, operands[i].dtype) for i in late]
    held += [pltpu.SemaphoreType.DMA((len(late),))] if late else []

    def space(i):
        if i in unread:
            return pl.ANY
        return pltpu.HBM if i in slow else pltpu.SMEM if i in smem else pltpu.VMEM

    return pl.pallas_call(
        body,
        out_shape=out_shape,
        in_specs=[pl.BlockSpec(memory_space=space(i)) for i in range(len(operands))],
        scratch_shapes=held + list(scratch),
        input_output_aliases=aliases,
        compiler_params=pltpu.CompilerParams(vmem_limit_bytes=16 << 20),
        cost_estimate=pl.CostEstimate(flops=(cost or 0) * 1000, bytes_accessed=cost or total, transcendentals=0),
        **extra,
    )(*given)


def positions(target, devices):
    count = target.shape[1]
    earlier = one_hot(iota((count, count), 0) < iota((count, count), 1))
    match = iota((devices, count), 0) == target
    before = dot(one_hot(match), earlier)
    return jnp.sum(jnp.where(match, before, 0.0), axis=0, keepdims=True).astype(jnp.int32)


def pack(sizes, half, target, seg, value, ocean, weight, out, staged, out_sems):
    devices, ocn_count, cap = sizes
    across = ocn_count // 2
    owners = devices // 2
    slots = owners * cap
    count = target.shape[1]
    chans, (segs, width) = len(ocean), ocean[0].shape
    stores = []

    def send(index, size, values):
        piece = pl.ds(index * cap, size)
        staged[:, piece, :] = values.reshape(owners, size, width)
        store = pltpu.make_async_copy(
            staged.at[:, piece, :], out.at[:, piece, :], out_sems.at[index]
        )
        store.start()
        stores.append(store)

    position = positions(target, devices)
    beside = target % ocn_count
    group = target // ocn_count * across + beside % across
    group = jnp.where(beside // across == half, group, owners)
    slot = group * cap + position
    place = one_hot(iota((slots, count), 0) == slot)
    member = one_hot(iota((segs, count), 0) == seg)
    of_seg = dot(place, member, (1, 1)).astype(BF16)
    for chan, sent in enumerate(exact_dots(of_seg, ocean)):
        send(chan, cap, sent)
    (reach,) = exact_dots(place, [weight])
    send(chans, cap, reach)
    line = iota((owners * EDGE, count), 0)
    tall = line == group * EDGE + (position & (EDGE - 1))
    flat = line == group * EDGE
    lane = iota((width, count), 0)
    tall_lane = lane == lax.shift_right_logical(position, EDGE.bit_length() - 1)
    flat_lane = lane == position + FLAT
    coarse, fine = lax.shift_right_logical(value, 5).astype(F32), (value & 31).astype(F32)
    lanes = jnp.concatenate(
        [
            jnp.concatenate([jnp.where(at, v, 0.0) for at in (tall_lane, flat_lane)], axis=1)
            for v in (coarse, fine)
        ],
        axis=0,
    ).astype(BF16)
    labels = dot(jnp.concatenate([one_hot(tall), one_hot(flat)], axis=1), lanes, (1, 1))
    send(chans + 1, EDGE, labels[:, :width] * 32.0 + labels[:, width:])
    return stores


def send_kernel(seg, mask, area, dest, row, ocean, sent):
    segs, width = mask.target.shape
    count = area.target.shape[0]
    lines = count // width
    chans = ocean.target.shape[0]
    first = chans * segs
    found = seg.get()[...]
    member = one_hot(iota((segs, count), 0) == found)
    sea = dot(member, mask.get()[...].astype(F32).astype(BF16), (0, 0))
    sent[first : first + count, :] = area.get()[...] * sea
    flat = [
        index[:, line * width : (line + 1) * width].astype(F32)
        for index in (dest.get()[...], found, row.get()[...])
        for line in range(lines)
    ]
    rest = sent.shape[0] - first - count - len(flat)
    sent[first + count :, :] = jnp.concatenate(flat + [jnp.zeros((rest, width), F32)], axis=0)
    values = ocean.get()
    for chan in range(chans):
        sent[chan * segs : (chan + 1) * segs, :] = values[chan]


def pack_kernel(sizes, count, chans, half, sent, out, staged, out_sems):
    width = sent.shape[1]
    lines = count // width
    rest = -(-3 * lines // 16) * 16
    segs = (sent.shape[0] - count - rest) // chans
    first = chans * segs + count

    def vector(index):
        at = first + index * lines
        pieces = [sent[at + line : at + line + 1, :] for line in range(lines)]
        return jnp.concatenate(pieces, axis=1).astype(jnp.int32)

    ocean = [sent[chan * segs : (chan + 1) * segs, :] for chan in range(chans)]
    weight = sent[chans * segs : first, :]
    indices = [vector(index) for index in range(3)]
    for copy in pack(sizes, half[0], *indices, ocean, weight, out, staged, out_sems):
        copy.wait()


def edge_lane(takes, width, high):
    def lane(line):
        at, first = jnp.full(line.shape, -1, jnp.int32), 0
        for index, take in enumerate(takes):
            inside = (line >= first) & (line < first + take)
            start = index * width + (width - take if high else 0)
            at = jnp.where(inside, start + line - first, at)
            first += take
        return at

    return lane


def strip_lane(first, chans, width):
    def lane(line):
        at, place = jnp.full(line.shape, -1, jnp.int32), line % STRIP
        start = (first + line // STRIP) * width
        low = (place >= ITERS) & (place < 3 * ITERS)
        high = (place >= 3 * ITERS) & (place < 5 * ITERS)
        at = jnp.where(low, start + place - ITERS, at)
        at = jnp.where(high, start + width + place - 5 * ITERS, at)
        return jnp.where(line < chans * STRIP, at, -1)

    return lane


def fill_strip(own, left, right, first, chans, take):
    pieces = []
    gap = [jnp.zeros((ITERS - take, own.shape[1]), F32)] if take < ITERS else []
    for chan in range(chans):
        beside = slice(first + chan * take, first + (chan + 1) * take)
        inner = slice(chan * STRIP + ITERS, (chan + 1) * STRIP - ITERS)
        pieces += gap + [left[beside, 0, :], own[inner, :], right[beside, 0, :]] + gap
    pieces.append(jnp.zeros((own.shape[0] - chans * STRIP, own.shape[1]), F32))
    return jnp.concatenate(pieces, axis=0)


def edge_columns(pieces, outputs):
    width = pieces[0][0].shape[1]
    length = outputs[0][0].shape[-1]
    tail = length - sum(piece.shape[0] for piece in pieces[0])
    whole = jnp.concatenate(
        [jnp.concatenate([*piece, jnp.zeros((tail, width), F32)], axis=0) for piece in pieces],
        axis=1,
    )
    rows = []
    for ref, lane in outputs:
        shape = (-(-ref.shape[0] // EDGE) * EDGE, whole.shape[1])
        rows.append(iota(shape, 1) == lane(iota(shape, 0)))
    select = one_hot(jnp.concatenate([row.astype(jnp.int32) for row in rows], axis=0) > 0)
    top, middle, bottom = split3(whole)
    edges = dot(select, bottom, (1, 1)) + dot(select, middle, (1, 1))
    edges = edges + dot(select, top, (1, 1))
    first = 0
    for ref, _ in outputs:
        ref[...] = edges[first : first + ref.shape[0]].reshape(ref.shape)
        first += -(-ref.shape[0] // EDGE) * EDGE


def first_columns_kernel(before, after, atm, diff, low, high, own):
    chans, _, width = atm.target.shape
    bodies = [ref.get()[chan] for ref in (atm, diff) for chan in range(chans)]
    takes = [1] * chans + [ITERS - 1] * chans
    pieces = [(before[i], body, after[i]) for i, body in enumerate(bodies)]
    edge_columns(
        pieces,
        [
            (low, edge_lane(takes, width, False)),
            (high, edge_lane(takes, width, True)),
            (own, strip_lane(chans, chans, width)),
        ],
    )


def columns_kernel(before, body, after, low, high, own):
    chans, _, width = body.shape
    pieces = [(before[i], body[i], after[i]) for i in range(chans)]
    edge_columns(
        pieces,
        [
            (low, edge_lane([ITERS] * chans, width, False)),
            (high, edge_lane([ITERS] * chans, width, True)),
            (own, strip_lane(0, chans, width)),
        ],
    )


def beside_rows(x):
    rows = x.shape[0]
    return pltpu.roll(x, rows - 1, 0) + pltpu.roll(x, 1, 0)


def beside_columns(x):
    width = x.shape[1]
    return pltpu.roll(x, width - 1, 1), pltpu.roll(x, 1, 1)


def beside_body(body, side=None):
    rows, width = body.shape
    lane = iota(body.shape, 1)
    east, west = beside_columns(body)
    east = jnp.where(lane == width - 1, 0.0 if side is None else side, east)
    west = jnp.where(lane == 0, 0.0 if side is None else side, west)
    return beside_rows(body) + east + west


def smooth_kernel(cap, before, after, left, right, atm, dest, seg, table, seg_select, held, sems):
    chans, rows, width = atm.target.shape
    segs, slots = held.shape
    target = dest.get()[...]
    slot = target * cap + positions(target, slots // cap)
    place = one_hot(iota((slots, target.shape[1]), 0) == slot)
    member = one_hot(iota((segs, target.shape[1]), 0) == seg.get()[...])
    held[...] = dot(member, place, (1, 1)).astype(BF16)
    stores = [pltpu.make_async_copy(held, seg_select, sems.at[0])]
    stores[0].start()
    sides = nearest_columns(left, right, width, chans)
    state = atm.get()
    parts = []
    for chan in range(chans):
        body = jnp.concatenate([before[chan], state[chan], after[chan]], axis=0)
        side = sides[: body.shape[0], chan * width : (chan + 1) * width]
        parts.append(split3((0.5 * body + 0.125 * beside_body(body, side))[EDGE : EDGE + rows]))
    table[...] = jnp.concatenate([p[level] for level in (2, 1, 0) for p in parts], axis=1)
    for store in stores:
        store.wait()


def nearest_columns(left, right, width, chans):
    edges = jnp.concatenate([left[:EDGE, 0, :], right[:EDGE, 0, :]], axis=0)
    shape = (6 * EDGE, chans * width)
    which, lane = iota(shape, 0), iota(shape, 1)
    line = which % (2 * EDGE)
    at = jnp.where(line < EDGE, line * width, (line - EDGE) * width + width - 1)
    select = one_hot((lane == at) & (line % EDGE < chans))
    return dot(jnp.concatenate(split3(edges), axis=0), select, (0, 0))


def flux_kernel(cap, ocn_count, mirrored, half, incoming, table, *rest):
    out, label_rows, staged, sems = rest[-4:]
    incoming = incoming if mirrored else incoming.get()
    owners, _, width = incoming.shape
    chans = staged.shape[1] // cap
    rows = table.shape[0]
    across = ocn_count // 2
    base = (1 - half[0] if mirrored else half[0]) * across
    groups = 4
    each = owners // groups
    stores = []
    label_rows[...] = incoming[:, (chans + 1) * cap, :]
    for group in range(groups):
        part_of = slice(group * each, (group + 1) * each)

        def part(index):
            piece = incoming[part_of, index * cap : (index + 1) * cap, :]
            return piece.reshape(each * cap, width)

        labels = incoming[part_of, (chans + 1) * cap :, :]
        labels = jnp.concatenate(
            [labels[i, :, j : j + 1] for i in range(each) for j in range(cap // EDGE)], axis=0
        ).astype(jnp.int32)
        select = one_hot(iota((each * cap, rows), 1) == labels)
        found = dot(select, table[...])
        pieces = [found[:, i * width : (i + 1) * width] for i in range(3 * chans)]
        air = [(pieces[i] + pieces[chans + i]) + pieces[2 * chans + i] for i in range(chans)]
        wind_east = air[1] - part(1)
        wind_north = air[2] - part(2)
        wind_speed = jnp.sqrt(wind_east * wind_east + wind_north * wind_north + 0.5)
        temp_gap = part(0) - air[0]
        factor = 1.0 + 0.5 * jnp.tanh(temp_gap / wind_speed)
        common = part(3) * factor * wind_speed
        for index, value in enumerate((0.8 * temp_gap, 0.6 * wind_east, 0.6 * wind_north)):
            staged[part_of, index * cap : (index + 1) * cap, :] = (common * value).reshape(
                each, cap, width
            )
        for line in range(group * each // across, (group + 1) * each // across):
            store = pltpu.make_async_copy(
                staged.at[pl.ds(line * across, across)],
                out.at[pl.ds(line * ocn_count + base, across)],
                sems.at[line],
            )
            store.start()
            stores.append(store)
    for store in stores:
        store.wait()


def forced_kernel(
    cap, ocn_count, half, own_labels, mirror_labels, weighted, atm, forced, top, bottom, held, sems
):
    owners, width = own_labels.shape
    devices = 2 * owners
    chans, rows, _ = forced.shape
    slots = devices * cap
    log = cap.bit_length() - 1
    across = ocn_count // 2
    loads = [
        pltpu.make_async_copy(
            weighted.at[pl.ds(line * ocn_count + base * across, across)],
            held.at[pl.ds(side * owners + line * across, across)],
            sems.at[side * (owners // across) + line],
        )
        for side, base in enumerate((half[0], 1 - half[0]))
        for line in range(owners // across)
    ]
    for load in loads:
        load.start()
    labels = jnp.concatenate([own_labels[...], mirror_labels[...]], axis=0).astype(jnp.int32)
    spread = one_hot(iota((width, slots), 0) == (iota((width, slots), 1) & (cap - 1)) + FLAT)
    coarse = dot(lax.shift_right_logical(labels, 5).astype(F32).astype(BF16), spread)
    fine = dot((labels & 31).astype(F32).astype(BF16), spread)
    owner = lax.shift_right_logical(iota((devices, slots), 1), log)
    label = jnp.where(owner == iota((devices, slots), 0), coarse * 32.0 + fine, 0.0)
    label = jnp.sum(label, axis=0, keepdims=True).astype(jnp.int32)
    select = one_hot(iota((rows, slots), 0) == label)
    state = atm.get()
    for load in loads:
        load.wait()
    values = [
        held[:, chan * cap : (chan + 1) * cap, :].reshape(slots, width) for chan in range(chans)
    ]
    for chan, air_sum in enumerate(exact_dots(select, values)):
        result = state[chan] + air_sum if chan == 0 else state[chan] - air_sum
        forced[chan] = result
        top[chan] = result[:EDGE]
        bottom[chan] = result[-EDGE:]


def diffuse_kernel(
    forced, before, after, diff_own, diff_left, diff_right, diff_before, diff_after, diff,
    out, diff_strip, staged, sems,
):
    chans, rows, width = forced.shape
    diff_strip[...] = fill_strip(diff_own, diff_left, diff_right, chans, chans, ITERS - 1)
    stores = []
    for chan in range(chans):
        body = jnp.concatenate([before[chan], forced[chan], after[chan]], axis=0)
        body_diff = [diff_before[chans + chan], diff.get()[chan], diff_after[chans + chan]]
        body_diff = jnp.concatenate(body_diff, axis=0)
        for _ in range(ITERS):
            body = body + body_diff * (beside_body(body) - 4.0 * body)
        staged[chan] = body[EDGE : EDGE + rows]
        stores.append(pltpu.make_async_copy(staged.at[chan], out.at[chan], sems.at[chan]))
        stores[-1].start()
    for store in stores:
        store.wait()


def finish_kernel(
    cap, returned, own, left, right, diff_strip, seg_select, inner, ocean_flux, atm_next,
    flux_staged, staged, sems,
):
    devices, _, width = returned.shape
    chans, rows, _ = staged.shape
    stores = []

    def send(source, target):
        stores.append(pltpu.make_async_copy(source, target, sems.at[len(stores)]))
        stores[-1].start()

    values = [
        returned[:, chan * cap : (chan + 1) * cap, :].reshape(devices * cap, width)
        for chan in range(chans)
    ]
    for chan, total in enumerate(exact_dots(seg_select.get()[...], values)):
        flux_staged[chan] = total
    send(flux_staged, ocean_flux)
    state = fill_strip(own, left, right, 0, chans, ITERS)
    spread = diff_strip[...]
    for _ in range(ITERS):
        east, west = beside_columns(state)
        state = state + spread * ((beside_rows(state) + east + west) - 4.0 * state)
    lines = state.shape[0]
    shape = (3 * lines, chans * width)
    which, lane = iota(shape, 0) % lines, iota(shape, 1)
    place, start = which % STRIP, which // STRIP * width
    low = (place >= ITERS) & (place < 2 * ITERS) & (lane == start + place - ITERS)
    high = (place >= 4 * ITERS) & (place < 5 * ITERS)
    high = high & (lane == start + width + place - 5 * ITERS)
    select = one_hot((which < chans * STRIP) & (low | high))
    edges = dot(jnp.concatenate(split3(state), axis=0), select, (0, 0))
    lane = iota((rows, width), 1)
    outer = (lane < ITERS) | (lane >= width - ITERS)
    middle = inner.get()
    for chan in range(chans):
        edge = edges[EDGE : EDGE + rows, chan * width : (chan + 1) * width]
        staged[chan] = jnp.where(outer, edge, middle[chan])
        send(staged.at[chan], atm_next.at[chan])
    for store in stores:
        store.wait()


def shift(axis, low_edge, high_edge):
    count = lax.axis_size(axis)
    forward = [(i, i + 1) for i in range(count - 1)]
    backward = [(target, source) for source, target in forward]
    return lax.ppermute(high_edge, axis, forward), lax.ppermute(low_edge, axis, backward)


def per_device(atm, diff, ocean, mask, area, seg, dest, row):
    atm_count, ocn_count = lax.axis_size("atm"), lax.axis_size("ocn")
    devices = atm_count * ocn_count
    rows, chans, width = atm.shape
    count = seg.shape[0]
    segs = ocean.shape[0]
    cap = max(2, 2 * count // devices)
    slots = devices * cap
    atm = jnp.transpose(atm, (1, 0, 2))
    diff = jnp.transpose(diff, (1, 0, 2))
    ocean = jnp.transpose(ocean, (1, 0, 2))

    def shape(*dims, dtype=F32):
        return jax.ShapeDtypeStruct(dims, dtype)

    hbm, fast = pltpu.HBM, pl.BlockSpec(memory_space=pltpu.VMEM)
    slow = pl.BlockSpec(memory_space=hbm)
    dest, seg, row = dest.reshape(1, count), seg.reshape(1, count), row.reshape(1, count)
    across = ocn_count // 2
    owners = devices // 2
    half = (lax.axis_index("ocn") // across).astype(jnp.int32).reshape(1)
    halves = [
        [i * ocn_count + side * across + j for i in range(atm_count) for j in range(across)]
        for side in range(2)
    ]
    mirror = [(j, (j + across) % ocn_count) for j in range(ocn_count)]
    sizes = (devices, ocn_count, cap)
    packed = (owners, (chans + 1) * cap + EDGE, width)
    lines_sent = chans * segs + count + -(-3 * count // width // 16) * 16

    def exchange(x):
        return lax.all_to_all(
            x, BOTH, split_axis=0, concat_axis=0, tiled=True, axis_index_groups=halves
        )

    sent = call(
        send_kernel,
        shape(lines_sent, width),
        (seg, mask, area, dest, row, ocean),
        late=(0, 1, 2, 3, 4, 5),
        cost=COST_SEND,
    )
    received = lax.ppermute(sent, "ocn", mirror)

    def packing(sent, cost, *ahead):
        return call(
            functools.partial(pack_kernel, sizes, count, chans),
            hbm(packed, F32),
            (half, sent),
            smem=(0,),
            after=ahead,
            outs=slow,
            scratch=[pltpu.VMEM(packed, F32), pltpu.SemaphoreType.DMA((chans + 2,))],
            cost=cost,
        )

    first = jnp.concatenate([atm[:, :EDGE], diff[:, :EDGE]], axis=0)
    final = jnp.concatenate([atm[:, -EDGE:], diff[:, -EDGE:]], axis=0)
    before, after = shift("atm", first, final)
    own_packed = packing(sent, COST_OWN)
    own_incoming = exchange(own_packed)
    long = -(-(rows + 2 * EDGE) // 128) * 128

    edge = shape(chans * ITERS, 1, long)

    def lines(columns):
        return shape(-(-columns // EDGE) * EDGE, long)

    low, high, diff_own = call(
        first_columns_kernel,
        (edge, edge, lines(chans * STRIP)),
        (before, after, atm, diff),
        late=(2, 3),
        after=(own_packed,),
        cost=COST_FIRST,
    )
    left, right = shift("ocn", low, high)
    mirror_packed = packing(received, COST_MIRROR, diff_own)
    mirror_incoming = exchange(mirror_packed)

    table, seg_select = call(
        functools.partial(smooth_kernel, cap),
        (pltpu.VMEM((rows, 3 * chans * width), BF16), hbm((segs, slots), BF16)),
        (before, after, left, right, atm, dest, seg),
        late=(4, 5, 6),
        after=(mirror_packed,),
        outs=(fast, slow),
        cost=COST_SMOOTH,
        scratch=[pltpu.VMEM((segs, slots), BF16), pltpu.SemaphoreType.DMA((1,))],
    )

    def flux(incoming, mirrored, begun):
        return call(
            functools.partial(flux_kernel, cap, ocn_count, mirrored),
            (
                hbm((devices, chans * cap, width), F32),
                shape(owners, width),
            ),
            (half, incoming, table, *begun),
            smem=(0,),
            late=() if mirrored else (1,),
            outs=(slow, fast),
            scratch=[
                pltpu.VMEM((owners, chans * cap, width), F32),
                pltpu.SemaphoreType.DMA((atm_count,)),
            ],
            aliases={3: 0} if begun else {},
        )

    begun, own_labels = flux(own_incoming, False, ())
    weighted, mirror_labels = flux(mirror_incoming, True, (begun,))
    returned = lax.all_to_all(weighted, BOTH, split_axis=0, concat_axis=0, tiled=True)
    forced, top, bottom = call(
        functools.partial(forced_kernel, cap, ocn_count),
        (
            pltpu.VMEM((chans, rows, width), F32),
            shape(chans, EDGE, width),
            shape(chans, EDGE, width),
        ),
        (half, own_labels, mirror_labels, weighted, atm),
        smem=(0,),
        plain=(3,),
        late=(4,),
        scratch=[
            pltpu.VMEM((devices, chans * cap, width), F32),
            pltpu.SemaphoreType.DMA((2 * atm_count,)),
        ],
    )
    forced_before, forced_after = shift("atm", top, bottom)
    forced_low, forced_high, forced_own = call(
        columns_kernel,
        (edge, edge, lines(chans * STRIP)),
        (forced_before, forced, forced_after),
    )
    forced_left, forced_right = shift("ocn", forced_low, forced_high)
    inner, diff_strip = call(
        diffuse_kernel,
        (hbm((chans, rows, width), F32), lines(chans * STRIP)),
        (forced, forced_before, forced_after, diff_own, left, right, before, after, diff),
        late=(8,),
        outs=(slow, fast),
        scratch=[pltpu.VMEM((chans, rows, width), F32), pltpu.SemaphoreType.DMA((chans,))],
    )
    ocean_flux, atm_next = call(
        functools.partial(finish_kernel, cap),
        (hbm((chans, segs, width), F32), hbm((chans, rows, width), F32)),
        (returned, forced_own, forced_left, forced_right, diff_strip, seg_select, inner),
        late=(5, 6),
        outs=(slow, slow),
        scratch=[
            pltpu.VMEM((chans, segs, width), F32),
            pltpu.VMEM((chans, rows, width), F32),
            pltpu.SemaphoreType.DMA((1 + chans,)),
        ],
    )
    return jnp.transpose(atm_next, (1, 0, 2)), jnp.transpose(ocean_flux, (1, 0, 2))


def solution(mesh):
    placed = (
        P("atm", None, "ocn"),
        P("atm", None, "ocn"),
        P(BOTH, None, None),
        P(BOTH, None),
        P(BOTH, None),
        P(BOTH),
        P(BOTH, None),
        P(BOTH),
    )
    return jax.shard_map(
        per_device,
        mesh=mesh,
        in_specs=placed,
        out_specs=(P("atm", None, "ocn"), P(BOTH, None, None)),
        check_vma=False,
    )
```

```python
import functools

import jax
import jax.numpy as jnp
from jax import lax
from jax.experimental import pallas as pl
from jax.experimental.pallas import tpu as pltpu
from jax.sharding import PartitionSpec as P

ITERS = 3
EDGE = 8
FLAT = 32
STRIP = 6 * ITERS
COST_SEND = 1 << 10
COST_OWN = 1 << 10
COST_MIRROR = 16 << 20
COST_FIRST = 1 << 10
COST_SMOOTH = 100 << 20
BOTH = ("atm", "ocn")
F32 = jnp.float32
BF16 = jnp.bfloat16


def split3(x):
    high = x.astype(BF16)
    rest = x - high.astype(F32)
    middle = rest.astype(BF16)
    low = (rest - middle.astype(F32)).astype(BF16)
    return high, middle, low


def dot(a, b, contract=(1, 0)):
    dims = (((contract[0],), (contract[1],)), ((), ()))
    return lax.dot_general(a, b, dims, preferred_element_type=F32)


def exact_dots(select, values, contract=(1, 0)):
    parts = [split3(x) for x in values]
    stacked = jnp.concatenate([p[level] for level in (2, 1, 0) for p in parts], axis=1)
    width, count = values[0].shape[1], len(values)
    result = dot(select, stacked, contract)

    def piece(level, index):
        at = (level * count + index) * width
        return result[:, at : at + width]

    return [(piece(0, i) + piece(1, i)) + piece(2, i) for i in range(count)]


def iota(shape, dim):
    return lax.broadcasted_iota(jnp.int32, shape, dim)


def one_hot(condition):
    return condition.astype(F32).astype(BF16)


class Late:
    def __init__(self, source, target, sem):
        self.target, self.copy = target, pltpu.make_async_copy(source, target, sem)
        self.copy.start()

    def get(self):
        if self.copy is not None:
            self.copy.wait()
            self.copy = None
        return self.target


def call(
    kernel, out_shape, operands, *, late=(), plain=(), smem=(), after=(), outs=None, cost=None, scratch=(), aliases={},
):
    total = sum(x.size * x.dtype.itemsize for x in operands)
    extra = {} if outs is None else {"out_specs": outs}
    count = len(operands)
    operands = [*operands, *after]
    unread = range(count, len(operands))
    slow = [*late, *plain, *aliases]
    given = [
        pltpu.with_memory_space_constraint(x, pltpu.HBM) if i in slow else x
        for i, x in enumerate(operands)
    ]
    results = len(jax.tree.leaves(out_shape))

    def body(*refs):
        first, second = len(operands), len(operands) + results
        inputs, held = list(refs[:count]), refs[second : second + len(late)]
        rest = refs[second + len(late) :]
        if late:
            sems, rest = rest[0], rest[1:]
            for at, i in enumerate(late):
                inputs[i] = Late(inputs[i], held[at], sems.at[at])
        kernel(*inputs, *refs[first:second], *rest)

    held = [pltpu.VMEM(operands[i].shape, operands[i].dtype) for i in late]
    held += [pltpu.SemaphoreType.DMA((len(late),))] if late else []

    def space(i):
        if i in unread:
            return pl.ANY
        return pltpu.HBM if i in slow else pltpu.SMEM if i in smem else pltpu.VMEM

    return pl.pallas_call(
        body,
        out_shape=out_shape,
        in_specs=[pl.BlockSpec(memory_space=space(i)) for i in range(len(operands))],
        scratch_shapes=held + list(scratch),
        input_output_aliases=aliases,
        compiler_params=pltpu.CompilerParams(vmem_limit_bytes=16 << 20),
        cost_estimate=pl.CostEstimate(flops=(cost or 0) * 1000, bytes_accessed=cost or total, transcendentals=0),
        **extra,
    )(*given)


def positions(target, devices):
    count = target.shape[1]
    earlier = one_hot(iota((count, count), 0) < iota((count, count), 1))
    match = iota((devices, count), 0) == target
    before = dot(one_hot(match), earlier)
    return jnp.sum(jnp.where(match, before, 0.0), axis=0, keepdims=True).astype(jnp.int32)


def pack(sizes, half, target, seg, value, ocean, weight, out, staged, out_sems):
    devices, ocn_count, cap = sizes
    across = ocn_count // 2
    owners = devices // 2
    slots = owners * cap
    count = target.shape[1]
    chans, (segs, width) = len(ocean), ocean[0].shape
    stores = []

    def send(index, size, values):
        piece = pl.ds(index * cap, size)
        staged[:, piece, :] = values.reshape(owners, size, width)
        store = pltpu.make_async_copy(
            staged.at[:, piece, :], out.at[:, piece, :], out_sems.at[index]
        )
        store.start()
        stores.append(store)

    position = positions(target, devices)
    beside = target % ocn_count
    group = target // ocn_count * across + beside % across
    group = jnp.where(beside // across == half, group, owners)
    slot = group * cap + position
    place = one_hot(iota((slots, count), 0) == slot)
    member = one_hot(iota((segs, count), 0) == seg)
    of_seg = dot(place, member, (1, 1)).astype(BF16)
    (reach,) = exact_dots(place, [weight])
    send(chans, cap, reach)
    for chan, sent in enumerate(exact_dots(of_seg, ocean)):
        send(chan, cap, sent)
    line = iota((owners * EDGE, count), 0)
    tall = line == group * EDGE + (position & (EDGE - 1))
    flat = line == group * EDGE
    lane = iota((width, count), 0)
    tall_lane = lane == lax.shift_right_logical(position, EDGE.bit_length() - 1)
    flat_lane = lane == position + FLAT
    coarse, fine = lax.shift_right_logical(value, 5).astype(F32), (value & 31).astype(F32)
    lanes = jnp.concatenate(
        [
            jnp.concatenate([jnp.where(at, v, 0.0) for at in (tall_lane, flat_lane)], axis=1)
            for v in (coarse, fine)
        ],
        axis=0,
    ).astype(BF16)
    labels = dot(jnp.concatenate([one_hot(tall), one_hot(flat)], axis=1), lanes, (1, 1))
    send(chans + 1, EDGE, labels[:, :width] * 32.0 + labels[:, width:])
    return stores


def send_kernel(seg, mask, area, dest, row, ocean, sent):
    segs, width = mask.target.shape
    count = area.target.shape[0]
    lines = count // width
    chans = ocean.target.shape[0]
    first = chans * segs
    found = seg.get()[...]
    member = one_hot(iota((segs, count), 0) == found)
    sea = dot(member, mask.get()[...].astype(F32).astype(BF16), (0, 0))
    sent[first : first + count, :] = area.get()[...] * sea
    flat = [
        index[:, line * width : (line + 1) * width].astype(F32)
        for index in (dest.get()[...], found, row.get()[...])
        for line in range(lines)
    ]
    rest = sent.shape[0] - first - count - len(flat)
    sent[first + count :, :] = jnp.concatenate(flat + [jnp.zeros((rest, width), F32)], axis=0)
    values = ocean.get()
    for chan in range(chans):
        sent[chan * segs : (chan + 1) * segs, :] = values[chan]


def pack_kernel(sizes, count, chans, half, sent, out, staged, out_sems):
    width = sent.shape[1]
    lines = count // width
    rest = -(-3 * lines // 16) * 16
    segs = (sent.shape[0] - count - rest) // chans
    first = chans * segs + count

    def vector(index):
        at = first + index * lines
        pieces = [sent[at + line : at + line + 1, :] for line in range(lines)]
        return jnp.concatenate(pieces, axis=1).astype(jnp.int32)

    ocean = [sent[chan * segs : (chan + 1) * segs, :] for chan in range(chans)]
    weight = sent[chans * segs : first, :]
    indices = [vector(index) for index in range(3)]
    for copy in pack(sizes, half[0], *indices, ocean, weight, out, staged, out_sems):
        copy.wait()


def edge_lane(takes, width, high):
    def lane(line):
        at, first = jnp.full(line.shape, -1, jnp.int32), 0
        for index, take in enumerate(takes):
            inside = (line >= first) & (line < first + take)
            start = index * width + (width - take if high else 0)
            at = jnp.where(inside, start + line - first, at)
            first += take
        return at

    return lane


def strip_lane(first, chans, width):
    def lane(line):
        at, place = jnp.full(line.shape, -1, jnp.int32), line % STRIP
        start = (first + line // STRIP) * width
        low = (place >= ITERS) & (place < 3 * ITERS)
        high = (place >= 3 * ITERS) & (place < 5 * ITERS)
        at = jnp.where(low, start + place - ITERS, at)
        at = jnp.where(high, start + width + place - 5 * ITERS, at)
        return jnp.where(line < chans * STRIP, at, -1)

    return lane


def fill_strip(own, left, right, first, chans, take):
    pieces = []
    gap = [jnp.zeros((ITERS - take, own.shape[1]), F32)] if take < ITERS else []
    for chan in range(chans):
        beside = slice(first + chan * take, first + (chan + 1) * take)
        inner = slice(chan * STRIP + ITERS, (chan + 1) * STRIP - ITERS)
        pieces += gap + [left[beside, 0, :], own[inner, :], right[beside, 0, :]] + gap
    pieces.append(jnp.zeros((own.shape[0] - chans * STRIP, own.shape[1]), F32))
    return jnp.concatenate(pieces, axis=0)


def edge_columns(pieces, outputs):
    width = pieces[0][0].shape[1]
    length = outputs[0][0].shape[-1]
    tail = length - sum(piece.shape[0] for piece in pieces[0])
    whole = jnp.concatenate(
        [jnp.concatenate([*piece, jnp.zeros((tail, width), F32)], axis=0) for piece in pieces],
        axis=1,
    )
    rows = []
    for ref, lane in outputs:
        shape = (-(-ref.shape[0] // EDGE) * EDGE, whole.shape[1])
        rows.append(iota(shape, 1) == lane(iota(shape, 0)))
    select = one_hot(jnp.concatenate([row.astype(jnp.int32) for row in rows], axis=0) > 0)
    top, middle, bottom = split3(whole)
    edges = dot(select, bottom, (1, 1)) + dot(select, middle, (1, 1))
    edges = edges + dot(select, top, (1, 1))
    first = 0
    for ref, _ in outputs:
        ref[...] = edges[first : first + ref.shape[0]].reshape(ref.shape)
        first += -(-ref.shape[0] // EDGE) * EDGE


def first_columns_kernel(before, after, atm, diff, low, high, own):
    chans, _, width = atm.target.shape
    bodies = [ref.get()[chan] for ref in (atm, diff) for chan in range(chans)]
    takes = [1] * chans + [ITERS - 1] * chans
    pieces = [(before[i], body, after[i]) for i, body in enumerate(bodies)]
    edge_columns(
        pieces,
        [
            (low, edge_lane(takes, width, False)),
            (high, edge_lane(takes, width, True)),
            (own, strip_lane(chans, chans, width)),
        ],
    )


def columns_kernel(before, body, after, low, high, own):
    chans, _, width = body.shape
    pieces = [(before[i], body[i], after[i]) for i in range(chans)]
    edge_columns(
        pieces,
        [
            (low, edge_lane([ITERS] * chans, width, False)),
            (high, edge_lane([ITERS] * chans, width, True)),
            (own, strip_lane(0, chans, width)),
        ],
    )


def beside_rows(x):
    rows = x.shape[0]
    return pltpu.roll(x, rows - 1, 0) + pltpu.roll(x, 1, 0)


def beside_columns(x):
    width = x.shape[1]
    return pltpu.roll(x, width - 1, 1), pltpu.roll(x, 1, 1)


def beside_body(body, side=None):
    rows, width = body.shape
    lane = iota(body.shape, 1)
    east, west = beside_columns(body)
    east = jnp.where(lane == width - 1, 0.0 if side is None else side, east)
    west = jnp.where(lane == 0, 0.0 if side is None else side, west)
    return beside_rows(body) + east + west


def smooth_kernel(cap, before, after, left, right, atm, dest, seg, table, seg_select, held, sems):
    chans, rows, width = atm.target.shape
    segs, slots = held.shape
    target = dest.get()[...]
    slot = target * cap + positions(target, slots // cap)
    place = one_hot(iota((slots, target.shape[1]), 0) == slot)
    member = one_hot(iota((segs, target.shape[1]), 0) == seg.get()[...])
    held[...] = dot(member, place, (1, 1)).astype(BF16)
    stores = [pltpu.make_async_copy(held, seg_select, sems.at[0])]
    stores[0].start()
    sides = nearest_columns(left, right, width, chans)
    state = atm.get()
    parts = []
    for chan in range(chans):
        body = jnp.concatenate([before[chan], state[chan], after[chan]], axis=0)
        side = sides[: body.shape[0], chan * width : (chan + 1) * width]
        parts.append(split3((0.5 * body + 0.125 * beside_body(body, side))[EDGE : EDGE + rows]))
    table[...] = jnp.concatenate([p[level] for level in (2, 1, 0) for p in parts], axis=1)
    for store in stores:
        store.wait()


def nearest_columns(left, right, width, chans):
    edges = jnp.concatenate([left[:EDGE, 0, :], right[:EDGE, 0, :]], axis=0)
    shape = (6 * EDGE, chans * width)
    which, lane = iota(shape, 0), iota(shape, 1)
    line = which % (2 * EDGE)
    at = jnp.where(line < EDGE, line * width, (line - EDGE) * width + width - 1)
    select = one_hot((lane == at) & (line % EDGE < chans))
    return dot(jnp.concatenate(split3(edges), axis=0), select, (0, 0))


def flux_kernel(cap, ocn_count, mirrored, half, incoming, table, *rest):
    out, label_rows, staged, sems = rest[-4:]
    incoming = incoming if mirrored else incoming.get()
    owners, _, width = incoming.shape
    chans = staged.shape[1] // cap
    rows = table.shape[0]
    across = ocn_count // 2
    base = (1 - half[0] if mirrored else half[0]) * across
    groups = 4
    each = owners // groups
    stores = []
    label_rows[...] = incoming[:, (chans + 1) * cap, :]
    for group in range(groups):
        part_of = slice(group * each, (group + 1) * each)

        def part(index):
            piece = incoming[part_of, index * cap : (index + 1) * cap, :]
            return piece.reshape(each * cap, width)

        labels = incoming[part_of, (chans + 1) * cap :, :]
        labels = jnp.concatenate(
            [labels[i, :, j : j + 1] for i in range(each) for j in range(cap // EDGE)], axis=0
        ).astype(jnp.int32)
        select = one_hot(iota((each * cap, rows), 1) == labels)
        found = dot(select, table[...])
        pieces = [found[:, i * width : (i + 1) * width] for i in range(3 * chans)]
        air = [(pieces[i] + pieces[chans + i]) + pieces[2 * chans + i] for i in range(chans)]
        wind_east = air[1] - part(1)
        wind_north = air[2] - part(2)
        wind_speed = jnp.sqrt(wind_east * wind_east + wind_north * wind_north + 0.5)
        temp_gap = part(0) - air[0]
        factor = 1.0 + 0.5 * jnp.tanh(temp_gap / wind_speed)
        common = part(3) * factor * wind_speed
        for index, value in enumerate((0.8 * temp_gap, 0.6 * wind_east, 0.6 * wind_north)):
            staged[part_of, index * cap : (index + 1) * cap, :] = (common * value).reshape(
                each, cap, width
            )
        for line in range(group * each // across, (group + 1) * each // across):
            store = pltpu.make_async_copy(
                staged.at[pl.ds(line * across, across)],
                out.at[pl.ds(line * ocn_count + base, across)],
                sems.at[line],
            )
            store.start()
            stores.append(store)
    for store in stores:
        store.wait()


def forced_kernel(
    cap, ocn_count, half, own_labels, mirror_labels, weighted, atm, forced, top, bottom, held, sems
):
    owners, width = own_labels.shape
    devices = 2 * owners
    chans, rows, _ = forced.shape
    slots = devices * cap
    log = cap.bit_length() - 1
    across = ocn_count // 2
    loads = [
        pltpu.make_async_copy(
            weighted.at[pl.ds(line * ocn_count + base * across, across)],
            held.at[pl.ds(side * owners + line * across, across)],
            sems.at[side * (owners // across) + line],
        )
        for side, base in enumerate((half[0], 1 - half[0]))
        for line in range(owners // across)
    ]
    for load in loads:
        load.start()
    labels = jnp.concatenate([own_labels[...], mirror_labels[...]], axis=0).astype(jnp.int32)
    spread = one_hot(iota((width, slots), 0) == (iota((width, slots), 1) & (cap - 1)) + FLAT)
    coarse = dot(lax.shift_right_logical(labels, 5).astype(F32).astype(BF16), spread)
    fine = dot((labels & 31).astype(F32).astype(BF16), spread)
    owner = lax.shift_right_logical(iota((devices, slots), 1), log)
    label = jnp.where(owner == iota((devices, slots), 0), coarse * 32.0 + fine, 0.0)
    label = jnp.sum(label, axis=0, keepdims=True).astype(jnp.int32)
    select = one_hot(iota((rows, slots), 0) == label)
    state = atm.get()
    for load in loads:
        load.wait()
    values = [
        held[:, chan * cap : (chan + 1) * cap, :].reshape(slots, width) for chan in range(chans)
    ]
    for chan, air_sum in enumerate(exact_dots(select, values)):
        result = state[chan] + air_sum if chan == 0 else state[chan] - air_sum
        forced[chan] = result
        top[chan] = result[:EDGE]
        bottom[chan] = result[-EDGE:]


def diffuse_kernel(
    forced, before, after, diff_own, diff_left, diff_right, diff_before, diff_after, diff,
    out, diff_strip, staged, sems,
):
    chans, rows, width = forced.shape
    diff_strip[...] = fill_strip(diff_own, diff_left, diff_right, chans, chans, ITERS - 1)
    stores = []
    for chan in range(chans):
        body = jnp.concatenate([before[chan], forced[chan], after[chan]], axis=0)
        body_diff = [diff_before[chans + chan], diff.get()[chan], diff_after[chans + chan]]
        body_diff = jnp.concatenate(body_diff, axis=0)
        for _ in range(ITERS):
            body = body + body_diff * (beside_body(body) - 4.0 * body)
        staged[chan] = body[EDGE : EDGE + rows]
        stores.append(pltpu.make_async_copy(staged.at[chan], out.at[chan], sems.at[chan]))
        stores[-1].start()
    for store in stores:
        store.wait()


def finish_kernel(
    cap, returned, own, left, right, diff_strip, seg_select, inner, ocean_flux, atm_next,
    flux_staged, staged, sems,
):
    devices, _, width = returned.shape
    chans, rows, _ = staged.shape
    stores = []

    def send(source, target):
        stores.append(pltpu.make_async_copy(source, target, sems.at[len(stores)]))
        stores[-1].start()

    values = [
        returned[:, chan * cap : (chan + 1) * cap, :].reshape(devices * cap, width)
        for chan in range(chans)
    ]
    select = seg_select.get()[...]
    for chan in range(chans):
        (flux_staged[chan],) = exact_dots(select, [values[chan]])
    send(flux_staged, ocean_flux)
    state = fill_strip(own, left, right, 0, chans, ITERS)
    spread = diff_strip[...]
    for _ in range(ITERS):
        east, west = beside_columns(state)
        state = state + spread * ((beside_rows(state) + east + west) - 4.0 * state)
    lines = state.shape[0]
    shape = (3 * lines, chans * width)
    which, lane = iota(shape, 0) % lines, iota(shape, 1)
    place, start = which % STRIP, which // STRIP * width
    low = (place >= ITERS) & (place < 2 * ITERS) & (lane == start + place - ITERS)
    high = (place >= 4 * ITERS) & (place < 5 * ITERS)
    high = high & (lane == start + width + place - 5 * ITERS)
    select = one_hot((which < chans * STRIP) & (low | high))
    edges = dot(jnp.concatenate(split3(state), axis=0), select, (0, 0))
    lane = iota((rows, width), 1)
    outer = (lane < ITERS) | (lane >= width - ITERS)
    middle = inner.get()
    for chan in range(chans):
        edge = edges[EDGE : EDGE + rows, chan * width : (chan + 1) * width]
        staged[chan] = jnp.where(outer, edge, middle[chan])
        send(staged.at[chan], atm_next.at[chan])
    for store in stores:
        store.wait()


def shift(axis, low_edge, high_edge):
    count = lax.axis_size(axis)
    forward = [(i, i + 1) for i in range(count - 1)]
    backward = [(target, source) for source, target in forward]
    return lax.ppermute(high_edge, axis, forward), lax.ppermute(low_edge, axis, backward)


def per_device(atm, diff, ocean, mask, area, seg, dest, row):
    atm_count, ocn_count = lax.axis_size("atm"), lax.axis_size("ocn")
    devices = atm_count * ocn_count
    rows, chans, width = atm.shape
    count = seg.shape[0]
    segs = ocean.shape[0]
    cap = max(2, 2 * count // devices)
    slots = devices * cap
    atm = jnp.transpose(atm, (1, 0, 2))
    diff = jnp.transpose(diff, (1, 0, 2))
    ocean = jnp.transpose(ocean, (1, 0, 2))

    def shape(*dims, dtype=F32):
        return jax.ShapeDtypeStruct(dims, dtype)

    hbm, fast = pltpu.HBM, pl.BlockSpec(memory_space=pltpu.VMEM)
    slow = pl.BlockSpec(memory_space=hbm)
    dest, seg, row = dest.reshape(1, count), seg.reshape(1, count), row.reshape(1, count)
    across = ocn_count // 2
    owners = devices // 2
    half = (lax.axis_index("ocn") // across).astype(jnp.int32).reshape(1)
    halves = [
        [i * ocn_count + side * across + j for i in range(atm_count) for j in range(across)]
        for side in range(2)
    ]
    mirror = [(j, (j + across) % ocn_count) for j in range(ocn_count)]
    sizes = (devices, ocn_count, cap)
    packed = (owners, (chans + 1) * cap + EDGE, width)
    lines_sent = chans * segs + count + -(-3 * count // width // 16) * 16

    def exchange(x):
        return lax.all_to_all(
            x, BOTH, split_axis=0, concat_axis=0, tiled=True, axis_index_groups=halves
        )

    sent = call(
        send_kernel,
        shape(lines_sent, width),
        (seg, mask, area, dest, row, ocean),
        late=(0, 1, 2, 3, 4, 5),
        cost=COST_SEND,
    )
    received = lax.ppermute(sent, "ocn", mirror)

    def packing(sent, cost, *ahead):
        return call(
            functools.partial(pack_kernel, sizes, count, chans),
            hbm(packed, F32),
            (half, sent),
            smem=(0,),
            after=ahead,
            outs=slow,
            scratch=[pltpu.VMEM(packed, F32), pltpu.SemaphoreType.DMA((chans + 2,))],
            cost=cost,
        )

    first = jnp.concatenate([atm[:, :EDGE], diff[:, :EDGE]], axis=0)
    final = jnp.concatenate([atm[:, -EDGE:], diff[:, -EDGE:]], axis=0)
    before, after = shift("atm", first, final)
    own_packed = packing(sent, COST_OWN)
    own_incoming = exchange(own_packed)
    long = -(-(rows + 2 * EDGE) // 128) * 128

    edge = shape(chans * ITERS, 1, long)

    def lines(columns):
        return shape(-(-columns // EDGE) * EDGE, long)

    low, high, diff_own = call(
        first_columns_kernel,
        (edge, edge, lines(chans * STRIP)),
        (before, after, atm, diff),
        late=(2, 3),
        after=(own_packed,),
        cost=COST_FIRST,
    )
    left, right = shift("ocn", low, high)
    mirror_packed = packing(received, COST_MIRROR, diff_own)
    mirror_incoming = exchange(mirror_packed)

    table, seg_select = call(
        functools.partial(smooth_kernel, cap),
        (pltpu.VMEM((rows, 3 * chans * width), BF16), hbm((segs, slots), BF16)),
        (before, after, left, right, atm, dest, seg),
        late=(4, 5, 6),
        after=(mirror_packed,),
        outs=(fast, slow),
        cost=COST_SMOOTH,
        scratch=[pltpu.VMEM((segs, slots), BF16), pltpu.SemaphoreType.DMA((1,))],
    )

    def flux(incoming, mirrored, begun):
        return call(
            functools.partial(flux_kernel, cap, ocn_count, mirrored),
            (
                hbm((devices, chans * cap, width), F32),
                shape(owners, width),
            ),
            (half, incoming, table, *begun),
            smem=(0,),
            late=() if mirrored else (1,),
            outs=(slow, fast),
            scratch=[
                pltpu.VMEM((owners, chans * cap, width), F32),
                pltpu.SemaphoreType.DMA((atm_count,)),
            ],
            aliases={3: 0} if begun else {},
        )

    begun, own_labels = flux(own_incoming, False, ())
    weighted, mirror_labels = flux(mirror_incoming, True, (begun,))
    returned = lax.all_to_all(weighted, BOTH, split_axis=0, concat_axis=0, tiled=True)
    forced, top, bottom = call(
        functools.partial(forced_kernel, cap, ocn_count),
        (
            pltpu.VMEM((chans, rows, width), F32),
            shape(chans, EDGE, width),
            shape(chans, EDGE, width),
        ),
        (half, own_labels, mirror_labels, weighted, atm),
        smem=(0,),
        plain=(3,),
        late=(4,),
        scratch=[
            pltpu.VMEM((devices, chans * cap, width), F32),
            pltpu.SemaphoreType.DMA((2 * atm_count,)),
        ],
    )
    forced_before, forced_after = shift("atm", top, bottom)
    forced_low, forced_high, forced_own = call(
        columns_kernel,
        (edge, edge, lines(chans * STRIP)),
        (forced_before, forced, forced_after),
    )
    forced_left, forced_right = shift("ocn", forced_low, forced_high)
    inner, diff_strip = call(
        diffuse_kernel,
        (hbm((chans, rows, width), F32), lines(chans * STRIP)),
        (forced, forced_before, forced_after, diff_own, left, right, before, after, diff),
        late=(8,),
        outs=(slow, fast),
        scratch=[pltpu.VMEM((chans, rows, width), F32), pltpu.SemaphoreType.DMA((chans,))],
    )
    ocean_flux, atm_next = call(
        functools.partial(finish_kernel, cap),
        (hbm((chans, segs, width), F32), hbm((chans, rows, width), F32)),
        (returned, forced_own, forced_left, forced_right, diff_strip, seg_select, inner),
        late=(5, 6),
        outs=(slow, slow),
        scratch=[
            pltpu.VMEM((chans, segs, width), F32),
            pltpu.VMEM((chans, rows, width), F32),
            pltpu.SemaphoreType.DMA((1 + chans,)),
        ],
    )
    return jnp.transpose(atm_next, (1, 0, 2)), jnp.transpose(ocean_flux, (1, 0, 2))


def solution(mesh):
    placed = (
        P("atm", None, "ocn"),
        P("atm", None, "ocn"),
        P(BOTH, None, None),
        P(BOTH, None),
        P(BOTH, None),
        P(BOTH),
        P(BOTH, None),
        P(BOTH),
    )
    return jax.shard_map(
        per_device,
        mesh=mesh,
        in_specs=placed,
        out_specs=(P("atm", None, "ocn"), P(BOTH, None, None)),
        check_vma=False,
    )
```

```python
import functools

import jax
import jax.numpy as jnp
from jax import lax
from jax.experimental import pallas as pl
from jax.experimental.pallas import tpu as pltpu
from jax.sharding import PartitionSpec as P

ITERS = 3
EDGE = 8
FLAT = 32
STRIP = 6 * ITERS
COST_SEND = 1 << 10
COST_OWN = 1 << 10
COST_MIRROR = 16 << 20
COST_FIRST = 1 << 10
COST_SMOOTH = 100 << 20
BOTH = ("atm", "ocn")
F32 = jnp.float32
BF16 = jnp.bfloat16


def split3(x):
    high = x.astype(BF16)
    rest = x - high.astype(F32)
    middle = rest.astype(BF16)
    low = (rest - middle.astype(F32)).astype(BF16)
    return high, middle, low


def dot(a, b, contract=(1, 0)):
    dims = (((contract[0],), (contract[1],)), ((), ()))
    return lax.dot_general(a, b, dims, preferred_element_type=F32)


def exact_dots(select, values, contract=(1, 0)):
    parts = [split3(x) for x in values]
    stacked = jnp.concatenate([p[level] for level in (2, 1, 0) for p in parts], axis=1)
    width, count = values[0].shape[1], len(values)
    result = dot(select, stacked, contract)

    def piece(level, index):
        at = (level * count + index) * width
        return result[:, at : at + width]

    return [(piece(0, i) + piece(1, i)) + piece(2, i) for i in range(count)]


def iota(shape, dim):
    return lax.broadcasted_iota(jnp.int32, shape, dim)


def one_hot(condition):
    return condition.astype(F32).astype(BF16)


class Late:
    def __init__(self, source, target, sem):
        self.target, self.copy = target, pltpu.make_async_copy(source, target, sem)
        self.copy.start()

    def get(self):
        if self.copy is not None:
            self.copy.wait()
            self.copy = None
        return self.target


def call(
    kernel, out_shape, operands, *, late=(), plain=(), smem=(), after=(), outs=None, cost=None, scratch=(), aliases={},
):
    total = sum(x.size * x.dtype.itemsize for x in operands)
    extra = {} if outs is None else {"out_specs": outs}
    count = len(operands)
    operands = [*operands, *after]
    unread = range(count, len(operands))
    slow = [*late, *plain, *aliases]
    given = [
        pltpu.with_memory_space_constraint(x, pltpu.HBM) if i in slow else x
        for i, x in enumerate(operands)
    ]
    results = len(jax.tree.leaves(out_shape))

    def body(*refs):
        first, second = len(operands), len(operands) + results
        inputs, held = list(refs[:count]), refs[second : second + len(late)]
        rest = refs[second + len(late) :]
        if late:
            sems, rest = rest[0], rest[1:]
            for at, i in enumerate(late):
                inputs[i] = Late(inputs[i], held[at], sems.at[at])
        kernel(*inputs, *refs[first:second], *rest)

    held = [pltpu.VMEM(operands[i].shape, operands[i].dtype) for i in late]
    held += [pltpu.SemaphoreType.DMA((len(late),))] if late else []

    def space(i):
        if i in unread:
            return pl.ANY
        return pltpu.HBM if i in slow else pltpu.SMEM if i in smem else pltpu.VMEM

    return pl.pallas_call(
        body,
        out_shape=out_shape,
        in_specs=[pl.BlockSpec(memory_space=space(i)) for i in range(len(operands))],
        scratch_shapes=held + list(scratch),
        input_output_aliases=aliases,
        compiler_params=pltpu.CompilerParams(vmem_limit_bytes=16 << 20),
        cost_estimate=pl.CostEstimate(flops=(cost or 0) * 1000, bytes_accessed=cost or total, transcendentals=0),
        **extra,
    )(*given)


def positions(target, devices):
    count = target.shape[1]
    earlier = one_hot(iota((count, count), 0) < iota((count, count), 1))
    match = iota((devices, count), 0) == target
    before = dot(one_hot(match), earlier)
    return jnp.sum(jnp.where(match, before, 0.0), axis=0, keepdims=True).astype(jnp.int32)


def pack(sizes, half, target, seg, value, ocean, weight, out, staged, out_sems):
    devices, ocn_count, cap = sizes
    across = ocn_count // 2
    owners = devices // 2
    slots = owners * cap
    count = target.shape[1]
    chans, (segs, width) = len(ocean), ocean[0].shape
    stores = []

    def send(index, size, values):
        piece = pl.ds(index * cap, size)
        staged[:, piece, :] = values.reshape(owners, size, width)
        store = pltpu.make_async_copy(
            staged.at[:, piece, :], out.at[:, piece, :], out_sems.at[index]
        )
        store.start()
        stores.append(store)

    position = positions(target, devices)
    beside = target % ocn_count
    group = target // ocn_count * across + beside % across
    group = jnp.where(beside // across == half, group, owners)
    slot = group * cap + position
    place = one_hot(iota((slots, count), 0) == slot)
    member = one_hot(iota((segs, count), 0) == seg)
    of_seg = dot(place, member, (1, 1)).astype(BF16)
    (reach,) = exact_dots(place, [weight])
    send(chans, cap, reach)
    for chan, sent in enumerate(exact_dots(of_seg, ocean)):
        send(chan, cap, sent)
    line = iota((owners * EDGE, count), 0)
    tall = line == group * EDGE + (position & (EDGE - 1))
    flat = line == group * EDGE
    lane = iota((width, count), 0)
    tall_lane = lane == lax.shift_right_logical(position, EDGE.bit_length() - 1)
    flat_lane = lane == position + FLAT
    coarse, fine = lax.shift_right_logical(value, 5).astype(F32), (value & 31).astype(F32)
    lanes = jnp.concatenate(
        [
            jnp.concatenate([jnp.where(at, v, 0.0) for at in (tall_lane, flat_lane)], axis=1)
            for v in (coarse, fine)
        ],
        axis=0,
    ).astype(BF16)
    labels = dot(jnp.concatenate([one_hot(tall), one_hot(flat)], axis=1), lanes, (1, 1))
    send(chans + 1, EDGE, labels[:, :width] * 32.0 + labels[:, width:])
    return stores


def send_kernel(seg, mask, area, dest, row, ocean, sent):
    segs, width = mask.target.shape
    count = area.target.shape[0]
    lines = count // width
    chans = ocean.target.shape[0]
    first = chans * segs
    found = seg.get()[...]
    member = one_hot(iota((segs, count), 0) == found)
    sea = dot(member, mask.get()[...].astype(F32).astype(BF16), (0, 0))
    sent[first : first + count, :] = area.get()[...] * sea
    flat = [
        index[:, line * width : (line + 1) * width].astype(F32)
        for index in (dest.get()[...], found, row.get()[...])
        for line in range(lines)
    ]
    rest = sent.shape[0] - first - count - len(flat)
    sent[first + count :, :] = jnp.concatenate(flat + [jnp.zeros((rest, width), F32)], axis=0)
    values = ocean.get()
    for chan in range(chans):
        sent[chan * segs : (chan + 1) * segs, :] = values[chan]


def pack_kernel(sizes, count, chans, half, sent, out, staged, out_sems):
    width = sent.shape[1]
    lines = count // width
    rest = -(-3 * lines // 16) * 16
    segs = (sent.shape[0] - count - rest) // chans
    first = chans * segs + count

    def vector(index):
        at = first + index * lines
        pieces = [sent[at + line : at + line + 1, :] for line in range(lines)]
        return jnp.concatenate(pieces, axis=1).astype(jnp.int32)

    ocean = [sent[chan * segs : (chan + 1) * segs, :] for chan in range(chans)]
    weight = sent[chans * segs : first, :]
    indices = [vector(index) for index in range(3)]
    for copy in pack(sizes, half[0], *indices, ocean, weight, out, staged, out_sems):
        copy.wait()


def edge_lane(takes, width, high):
    def lane(line):
        at, first = jnp.full(line.shape, -1, jnp.int32), 0
        for index, take in enumerate(takes):
            inside = (line >= first) & (line < first + take)
            start = index * width + (width - take if high else 0)
            at = jnp.where(inside, start + line - first, at)
            first += take
        return at

    return lane


def strip_lane(first, chans, width):
    def lane(line):
        at, place = jnp.full(line.shape, -1, jnp.int32), line % STRIP
        start = (first + line // STRIP) * width
        low = (place >= ITERS) & (place < 3 * ITERS)
        high = (place >= 3 * ITERS) & (place < 5 * ITERS)
        at = jnp.where(low, start + place - ITERS, at)
        at = jnp.where(high, start + width + place - 5 * ITERS, at)
        return jnp.where(line < chans * STRIP, at, -1)

    return lane


def fill_strip(own, left, right, first, chans, take):
    pieces = []
    gap = [jnp.zeros((ITERS - take, own.shape[1]), F32)] if take < ITERS else []
    for chan in range(chans):
        beside = slice(first + chan * take, first + (chan + 1) * take)
        inner = slice(chan * STRIP + ITERS, (chan + 1) * STRIP - ITERS)
        pieces += gap + [left[beside, 0, :], own[inner, :], right[beside, 0, :]] + gap
    pieces.append(jnp.zeros((own.shape[0] - chans * STRIP, own.shape[1]), F32))
    return jnp.concatenate(pieces, axis=0)


def edge_columns(pieces, outputs):
    width = pieces[0][0].shape[1]
    length = outputs[0][0].shape[-1]
    tail = length - sum(piece.shape[0] for piece in pieces[0])
    whole = jnp.concatenate(
        [jnp.concatenate([*piece, jnp.zeros((tail, width), F32)], axis=0) for piece in pieces],
        axis=1,
    )
    rows = []
    for ref, lane in outputs:
        shape = (-(-ref.shape[0] // EDGE) * EDGE, whole.shape[1])
        rows.append(iota(shape, 1) == lane(iota(shape, 0)))
    select = one_hot(jnp.concatenate([row.astype(jnp.int32) for row in rows], axis=0) > 0)
    top, middle, bottom = split3(whole)
    edges = dot(select, bottom, (1, 1)) + dot(select, middle, (1, 1))
    edges = edges + dot(select, top, (1, 1))
    first = 0
    for ref, _ in outputs:
        ref[...] = edges[first : first + ref.shape[0]].reshape(ref.shape)
        first += -(-ref.shape[0] // EDGE) * EDGE


def first_columns_kernel(before, after, atm, diff, low, high, own):
    chans, _, width = atm.target.shape
    bodies = [ref.get()[chan] for ref in (atm, diff) for chan in range(chans)]
    takes = [1] * chans + [ITERS - 1] * chans
    pieces = [(before[i], body, after[i]) for i, body in enumerate(bodies)]
    edge_columns(
        pieces,
        [
            (low, edge_lane(takes, width, False)),
            (high, edge_lane(takes, width, True)),
            (own, strip_lane(chans, chans, width)),
        ],
    )


def columns_kernel(before, body, after, low, high, own):
    chans, _, width = body.shape
    pieces = [(before[i], body[i], after[i]) for i in range(chans)]
    edge_columns(
        pieces,
        [
            (low, edge_lane([ITERS] * chans, width, False)),
            (high, edge_lane([ITERS] * chans, width, True)),
            (own, strip_lane(0, chans, width)),
        ],
    )


def beside_rows(x):
    rows = x.shape[0]
    return pltpu.roll(x, rows - 1, 0) + pltpu.roll(x, 1, 0)


def beside_columns(x):
    width = x.shape[1]
    return pltpu.roll(x, width - 1, 1), pltpu.roll(x, 1, 1)


def beside_body(body, side=None):
    rows, width = body.shape
    lane = iota(body.shape, 1)
    east, west = beside_columns(body)
    east = jnp.where(lane == width - 1, 0.0 if side is None else side, east)
    west = jnp.where(lane == 0, 0.0 if side is None else side, west)
    return beside_rows(body) + east + west


def smooth_kernel(cap, before, after, left, right, atm, dest, seg, table, seg_select, held, sems):
    chans, rows, width = atm.target.shape
    segs, slots = held.shape
    target = dest.get()[...]
    slot = target * cap + positions(target, slots // cap)
    place = one_hot(iota((slots, target.shape[1]), 0) == slot)
    member = one_hot(iota((segs, target.shape[1]), 0) == seg.get()[...])
    held[...] = dot(member, place, (1, 1)).astype(BF16)
    stores = [pltpu.make_async_copy(held, seg_select, sems.at[0])]
    stores[0].start()
    sides = nearest_columns(left, right, width, chans)
    state = atm.get()
    parts = []
    for chan in range(chans):
        body = jnp.concatenate([before[chan], state[chan], after[chan]], axis=0)
        side = sides[: body.shape[0], chan * width : (chan + 1) * width]
        parts.append(split3((0.5 * body + 0.125 * beside_body(body, side))[EDGE : EDGE + rows]))
    table[...] = jnp.concatenate([p[level] for level in (2, 1, 0) for p in parts], axis=1)
    for store in stores:
        store.wait()


def nearest_columns(left, right, width, chans):
    edges = jnp.concatenate([left[:EDGE, 0, :], right[:EDGE, 0, :]], axis=0)
    shape = (6 * EDGE, chans * width)
    which, lane = iota(shape, 0), iota(shape, 1)
    line = which % (2 * EDGE)
    at = jnp.where(line < EDGE, line * width, (line - EDGE) * width + width - 1)
    select = one_hot((lane == at) & (line % EDGE < chans))
    return dot(jnp.concatenate(split3(edges), axis=0), select, (0, 0))


def flux_kernel(cap, ocn_count, mirrored, half, incoming, table, *rest):
    out, label_rows, staged, sems = rest[-4:]
    incoming = incoming if mirrored else incoming.get()
    owners, _, width = incoming.shape
    chans = staged.shape[1] // cap
    rows = table.shape[0]
    across = ocn_count // 2
    base = (1 - half[0] if mirrored else half[0]) * across
    groups = 4
    each = owners // groups
    stores = []
    label_rows[...] = incoming[:, (chans + 1) * cap, :]
    for group in range(groups):
        part_of = slice(group * each, (group + 1) * each)

        def part(index):
            piece = incoming[part_of, index * cap : (index + 1) * cap, :]
            return piece.reshape(each * cap, width)

        labels = incoming[part_of, (chans + 1) * cap :, :]
        labels = jnp.concatenate(
            [labels[i, :, j : j + 1] for i in range(each) for j in range(cap // EDGE)], axis=0
        ).astype(jnp.int32)
        select = one_hot(iota((each * cap, rows), 1) == labels)
        found = dot(select, table[...])
        pieces = [found[:, i * width : (i + 1) * width] for i in range(3 * chans)]
        air = [(pieces[i] + pieces[chans + i]) + pieces[2 * chans + i] for i in range(chans)]
        wind_east = air[1] - part(1)
        wind_north = air[2] - part(2)
        wind_speed = jnp.sqrt(wind_east * wind_east + wind_north * wind_north + 0.5)
        temp_gap = part(0) - air[0]
        factor = 1.0 + 0.5 * jnp.tanh(temp_gap / wind_speed)
        common = part(3) * factor * wind_speed
        for index, value in enumerate((0.8 * temp_gap, 0.6 * wind_east, 0.6 * wind_north)):
            staged[part_of, index * cap : (index + 1) * cap, :] = (common * value).reshape(
                each, cap, width
            )
        for line in range(group * each // across, (group + 1) * each // across):
            store = pltpu.make_async_copy(
                staged.at[pl.ds(line * across, across)],
                out.at[pl.ds(line * ocn_count + base, across)],
                sems.at[line],
            )
            store.start()
            stores.append(store)
    for store in stores:
        store.wait()


def forced_kernel(
    cap, ocn_count, half, own_labels, mirror_labels, weighted, atm, forced, top, bottom, held, sems
):
    owners, width = own_labels.shape
    devices = 2 * owners
    chans, rows, _ = forced.shape
    slots = devices * cap
    log = cap.bit_length() - 1
    across = ocn_count // 2
    loads = [
        pltpu.make_async_copy(
            weighted.at[pl.ds(line * ocn_count + base * across, across)],
            held.at[pl.ds(side * owners + line * across, across)],
            sems.at[side * (owners // across) + line],
        )
        for side, base in enumerate((half[0], 1 - half[0]))
        for line in range(owners // across)
    ]
    for load in loads:
        load.start()
    labels = jnp.concatenate([own_labels[...], mirror_labels[...]], axis=0).astype(jnp.int32)
    spread = one_hot(iota((width, slots), 0) == (iota((width, slots), 1) & (cap - 1)) + FLAT)
    coarse = dot(lax.shift_right_logical(labels, 5).astype(F32).astype(BF16), spread)
    fine = dot((labels & 31).astype(F32).astype(BF16), spread)
    owner = lax.shift_right_logical(iota((devices, slots), 1), log)
    label = jnp.where(owner == iota((devices, slots), 0), coarse * 32.0 + fine, 0.0)
    label = jnp.sum(label, axis=0, keepdims=True).astype(jnp.int32)
    select = one_hot(iota((rows, slots), 0) == label)
    state = atm.get()
    for load in loads:
        load.wait()
    values = [
        held[:, chan * cap : (chan + 1) * cap, :].reshape(slots, width) for chan in range(chans)
    ]
    for chan in range(chans):
        (air_sum,) = exact_dots(select, [values[chan]])
        result = state[chan] + air_sum if chan == 0 else state[chan] - air_sum
        forced[chan] = result
        top[chan] = result[:EDGE]
        bottom[chan] = result[-EDGE:]


def diffuse_kernel(
    forced, before, after, diff_own, diff_left, diff_right, diff_before, diff_after, diff,
    out, diff_strip, staged, sems,
):
    chans, rows, width = forced.shape
    diff_strip[...] = fill_strip(diff_own, diff_left, diff_right, chans, chans, ITERS - 1)
    stores = []
    for chan in range(chans):
        body = jnp.concatenate([before[chan], forced[chan], after[chan]], axis=0)
        body_diff = [diff_before[chans + chan], diff.get()[chan], diff_after[chans + chan]]
        body_diff = jnp.concatenate(body_diff, axis=0)
        for _ in range(ITERS):
            body = body + body_diff * (beside_body(body) - 4.0 * body)
        staged[chan] = body[EDGE : EDGE + rows]
        stores.append(pltpu.make_async_copy(staged.at[chan], out.at[chan], sems.at[chan]))
        stores[-1].start()
    for store in stores:
        store.wait()


def finish_kernel(
    cap, returned, own, left, right, diff_strip, seg_select, inner, ocean_flux, atm_next,
    flux_staged, staged, sems,
):
    devices, _, width = returned.shape
    chans, rows, _ = staged.shape
    stores = []

    def send(source, target):
        stores.append(pltpu.make_async_copy(source, target, sems.at[len(stores)]))
        stores[-1].start()

    values = [
        returned[:, chan * cap : (chan + 1) * cap, :].reshape(devices * cap, width)
        for chan in range(chans)
    ]
    select = seg_select.get()[...]
    for chan in range(chans):
        (flux_staged[chan],) = exact_dots(select, [values[chan]])
    send(flux_staged, ocean_flux)
    state = fill_strip(own, left, right, 0, chans, ITERS)
    spread = diff_strip[...]
    for _ in range(ITERS):
        east, west = beside_columns(state)
        state = state + spread * ((beside_rows(state) + east + west) - 4.0 * state)
    lines = state.shape[0]
    shape = (3 * lines, chans * width)
    which, lane = iota(shape, 0) % lines, iota(shape, 1)
    place, start = which % STRIP, which // STRIP * width
    low = (place >= ITERS) & (place < 2 * ITERS) & (lane == start + place - ITERS)
    high = (place >= 4 * ITERS) & (place < 5 * ITERS)
    high = high & (lane == start + width + place - 5 * ITERS)
    select = one_hot((which < chans * STRIP) & (low | high))
    edges = dot(jnp.concatenate(split3(state), axis=0), select, (0, 0))
    lane = iota((rows, width), 1)
    outer = (lane < ITERS) | (lane >= width - ITERS)
    middle = inner.get()
    for chan in range(chans):
        edge = edges[EDGE : EDGE + rows, chan * width : (chan + 1) * width]
        staged[chan] = jnp.where(outer, edge, middle[chan])
        send(staged.at[chan], atm_next.at[chan])
    for store in stores:
        store.wait()


def shift(axis, low_edge, high_edge):
    count = lax.axis_size(axis)
    forward = [(i, i + 1) for i in range(count - 1)]
    backward = [(target, source) for source, target in forward]
    return lax.ppermute(high_edge, axis, forward), lax.ppermute(low_edge, axis, backward)


def per_device(atm, diff, ocean, mask, area, seg, dest, row):
    atm_count, ocn_count = lax.axis_size("atm"), lax.axis_size("ocn")
    devices = atm_count * ocn_count
    rows, chans, width = atm.shape
    count = seg.shape[0]
    segs = ocean.shape[0]
    cap = max(2, 2 * count // devices)
    slots = devices * cap
    atm = jnp.transpose(atm, (1, 0, 2))
    diff = jnp.transpose(diff, (1, 0, 2))
    ocean = jnp.transpose(ocean, (1, 0, 2))

    def shape(*dims, dtype=F32):
        return jax.ShapeDtypeStruct(dims, dtype)

    hbm, fast = pltpu.HBM, pl.BlockSpec(memory_space=pltpu.VMEM)
    slow = pl.BlockSpec(memory_space=hbm)
    dest, seg, row = dest.reshape(1, count), seg.reshape(1, count), row.reshape(1, count)
    across = ocn_count // 2
    owners = devices // 2
    half = (lax.axis_index("ocn") // across).astype(jnp.int32).reshape(1)
    halves = [
        [i * ocn_count + side * across + j for i in range(atm_count) for j in range(across)]
        for side in range(2)
    ]
    mirror = [(j, (j + across) % ocn_count) for j in range(ocn_count)]
    sizes = (devices, ocn_count, cap)
    packed = (owners, (chans + 1) * cap + EDGE, width)
    lines_sent = chans * segs + count + -(-3 * count // width // 16) * 16

    def exchange(x):
        return lax.all_to_all(
            x, BOTH, split_axis=0, concat_axis=0, tiled=True, axis_index_groups=halves
        )

    sent = call(
        send_kernel,
        shape(lines_sent, width),
        (seg, mask, area, dest, row, ocean),
        late=(0, 1, 2, 3, 4, 5),
        cost=COST_SEND,
    )
    received = lax.ppermute(sent, "ocn", mirror)

    def packing(sent, cost, *ahead):
        return call(
            functools.partial(pack_kernel, sizes, count, chans),
            hbm(packed, F32),
            (half, sent),
            smem=(0,),
            after=ahead,
            outs=slow,
            scratch=[pltpu.VMEM(packed, F32), pltpu.SemaphoreType.DMA((chans + 2,))],
            cost=cost,
        )

    first = jnp.concatenate([atm[:, :EDGE], diff[:, :EDGE]], axis=0)
    final = jnp.concatenate([atm[:, -EDGE:], diff[:, -EDGE:]], axis=0)
    before, after = shift("atm", first, final)
    own_packed = packing(sent, COST_OWN)
    own_incoming = exchange(own_packed)
    long = -(-(rows + 2 * EDGE) // 128) * 128

    edge = shape(chans * ITERS, 1, long)

    def lines(columns):
        return shape(-(-columns // EDGE) * EDGE, long)

    low, high, diff_own = call(
        first_columns_kernel,
        (edge, edge, lines(chans * STRIP)),
        (before, after, atm, diff),
        late=(2, 3),
        after=(own_packed,),
        cost=COST_FIRST,
    )
    left, right = shift("ocn", low, high)
    mirror_packed = packing(received, COST_MIRROR, diff_own)
    mirror_incoming = exchange(mirror_packed)

    table, seg_select = call(
        functools.partial(smooth_kernel, cap),
        (pltpu.VMEM((rows, 3 * chans * width), BF16), hbm((segs, slots), BF16)),
        (before, after, left, right, atm, dest, seg),
        late=(4, 5, 6),
        after=(mirror_packed,),
        outs=(fast, slow),
        cost=COST_SMOOTH,
        scratch=[pltpu.VMEM((segs, slots), BF16), pltpu.SemaphoreType.DMA((1,))],
    )

    def flux(incoming, mirrored, begun):
        return call(
            functools.partial(flux_kernel, cap, ocn_count, mirrored),
            (
                hbm((devices, chans * cap, width), F32),
                shape(owners, width),
            ),
            (half, incoming, table, *begun),
            smem=(0,),
            late=() if mirrored else (1,),
            outs=(slow, fast),
            scratch=[
                pltpu.VMEM((owners, chans * cap, width), F32),
                pltpu.SemaphoreType.DMA((atm_count,)),
            ],
            aliases={3: 0} if begun else {},
        )

    begun, own_labels = flux(own_incoming, False, ())
    weighted, mirror_labels = flux(mirror_incoming, True, (begun,))
    returned = lax.all_to_all(weighted, BOTH, split_axis=0, concat_axis=0, tiled=True)
    forced, top, bottom = call(
        functools.partial(forced_kernel, cap, ocn_count),
        (
            pltpu.VMEM((chans, rows, width), F32),
            shape(chans, EDGE, width),
            shape(chans, EDGE, width),
        ),
        (half, own_labels, mirror_labels, weighted, atm),
        smem=(0,),
        plain=(3,),
        late=(4,),
        scratch=[
            pltpu.VMEM((devices, chans * cap, width), F32),
            pltpu.SemaphoreType.DMA((2 * atm_count,)),
        ],
    )
    forced_before, forced_after = shift("atm", top, bottom)
    forced_low, forced_high, forced_own = call(
        columns_kernel,
        (edge, edge, lines(chans * STRIP)),
        (forced_before, forced, forced_after),
    )
    forced_left, forced_right = shift("ocn", forced_low, forced_high)
    inner, diff_strip = call(
        diffuse_kernel,
        (hbm((chans, rows, width), F32), lines(chans * STRIP)),
        (forced, forced_before, forced_after, diff_own, left, right, before, after, diff),
        late=(8,),
        outs=(slow, fast),
        scratch=[pltpu.VMEM((chans, rows, width), F32), pltpu.SemaphoreType.DMA((chans,))],
    )
    ocean_flux, atm_next = call(
        functools.partial(finish_kernel, cap),
        (hbm((chans, segs, width), F32), hbm((chans, rows, width), F32)),
        (returned, forced_own, forced_left, forced_right, diff_strip, seg_select, inner),
        late=(5, 6),
        outs=(slow, slow),
        scratch=[
            pltpu.VMEM((chans, segs, width), F32),
            pltpu.VMEM((chans, rows, width), F32),
            pltpu.SemaphoreType.DMA((1 + chans,)),
        ],
    )
    return jnp.transpose(atm_next, (1, 0, 2)), jnp.transpose(ocean_flux, (1, 0, 2))


def solution(mesh):
    placed = (
        P("atm", None, "ocn"),
        P("atm", None, "ocn"),
        P(BOTH, None, None),
        P(BOTH, None),
        P(BOTH, None),
        P(BOTH),
        P(BOTH, None),
        P(BOTH),
    )
    return jax.shard_map(
        per_device,
        mesh=mesh,
        in_specs=placed,
        out_specs=(P("atm", None, "ocn"), P(BOTH, None, None)),
        check_vma=False,
    )
```

```python
import functools

import jax
import jax.numpy as jnp
from jax import lax
from jax.experimental import pallas as pl
from jax.experimental.pallas import tpu as pltpu
from jax.sharding import PartitionSpec as P

ITERS = 3
EDGE = 8
FLAT = 32
STRIP = 6 * ITERS
COST_SEND = 1 << 10
COST_OWN = 1 << 10
COST_MIRROR = 16 << 20
COST_FIRST = 1 << 10
COST_SMOOTH = 100 << 20
BOTH = ("atm", "ocn")
F32 = jnp.float32
BF16 = jnp.bfloat16


def split3(x):
    high = x.astype(BF16)
    rest = x - high.astype(F32)
    middle = rest.astype(BF16)
    low = (rest - middle.astype(F32)).astype(BF16)
    return high, middle, low


def dot(a, b, contract=(1, 0)):
    dims = (((contract[0],), (contract[1],)), ((), ()))
    return lax.dot_general(a, b, dims, preferred_element_type=F32)


def exact_dots(select, values, contract=(1, 0)):
    parts = [split3(x) for x in values]
    stacked = jnp.concatenate([p[level] for level in (2, 1, 0) for p in parts], axis=1)
    width, count = values[0].shape[1], len(values)
    result = dot(select, stacked, contract)

    def piece(level, index):
        at = (level * count + index) * width
        return result[:, at : at + width]

    return [(piece(0, i) + piece(1, i)) + piece(2, i) for i in range(count)]


def iota(shape, dim):
    return lax.broadcasted_iota(jnp.int32, shape, dim)


def one_hot(condition):
    return condition.astype(F32).astype(BF16)


class Late:
    def __init__(self, source, target, sem):
        self.target, self.copy = target, pltpu.make_async_copy(source, target, sem)
        self.copy.start()

    def get(self):
        if self.copy is not None:
            self.copy.wait()
            self.copy = None
        return self.target


def call(
    kernel, out_shape, operands, *, late=(), plain=(), smem=(), after=(), outs=None, cost=None, scratch=(), aliases={},
):
    total = sum(x.size * x.dtype.itemsize for x in operands)
    extra = {} if outs is None else {"out_specs": outs}
    count = len(operands)
    operands = [*operands, *after]
    unread = range(count, len(operands))
    slow = [*late, *plain, *aliases]
    given = [
        pltpu.with_memory_space_constraint(x, pltpu.HBM) if i in slow else x
        for i, x in enumerate(operands)
    ]
    results = len(jax.tree.leaves(out_shape))

    def body(*refs):
        first, second = len(operands), len(operands) + results
        inputs, held = list(refs[:count]), refs[second : second + len(late)]
        rest = refs[second + len(late) :]
        if late:
            sems, rest = rest[0], rest[1:]
            for at, i in enumerate(late):
                inputs[i] = Late(inputs[i], held[at], sems.at[at])
        kernel(*inputs, *refs[first:second], *rest)

    held = [pltpu.VMEM(operands[i].shape, operands[i].dtype) for i in late]
    held += [pltpu.SemaphoreType.DMA((len(late),))] if late else []

    def space(i):
        if i in unread:
            return pl.ANY
        return pltpu.HBM if i in slow else pltpu.SMEM if i in smem else pltpu.VMEM

    return pl.pallas_call(
        body,
        out_shape=out_shape,
        in_specs=[pl.BlockSpec(memory_space=space(i)) for i in range(len(operands))],
        scratch_shapes=held + list(scratch),
        input_output_aliases=aliases,
        compiler_params=pltpu.CompilerParams(vmem_limit_bytes=16 << 20),
        cost_estimate=pl.CostEstimate(flops=(cost or 0) * 1000, bytes_accessed=cost or total, transcendentals=0),
        **extra,
    )(*given)


def positions(target, devices):
    count = target.shape[1]
    earlier = one_hot(iota((count, count), 0) < iota((count, count), 1))
    match = iota((devices, count), 0) == target
    before = dot(one_hot(match), earlier)
    return jnp.sum(jnp.where(match, before, 0.0), axis=0, keepdims=True).astype(jnp.int32)


def pack(sizes, half, target, seg, value, ocean, weight, out, staged, out_sems):
    devices, ocn_count, cap = sizes
    across = ocn_count // 2
    owners = devices // 2
    slots = owners * cap
    count = target.shape[1]
    chans, (segs, width) = len(ocean), ocean[0].shape
    stores = []

    def send(index, size, values):
        piece = pl.ds(index * cap, size)
        staged[:, piece, :] = values.reshape(owners, size, width)
        store = pltpu.make_async_copy(
            staged.at[:, piece, :], out.at[:, piece, :], out_sems.at[index]
        )
        store.start()
        stores.append(store)

    position = positions(target, devices)
    beside = target % ocn_count
    group = target // ocn_count * across + beside % across
    group = jnp.where(beside // across == half, group, owners)
    slot = group * cap + position
    place = one_hot(iota((slots, count), 0) == slot)
    member = one_hot(iota((segs, count), 0) == seg)
    of_seg = dot(place, member, (1, 1)).astype(BF16)
    (reach,) = exact_dots(place, [weight])
    send(chans, cap, reach)
    line = iota((owners * EDGE, count), 0)
    tall = line == group * EDGE + (position & (EDGE - 1))
    flat = line == group * EDGE
    lane = iota((width, count), 0)
    tall_lane = lane == lax.shift_right_logical(position, EDGE.bit_length() - 1)
    flat_lane = lane == position + FLAT
    coarse, fine = lax.shift_right_logical(value, 5).astype(F32), (value & 31).astype(F32)
    lanes = jnp.concatenate(
        [
            jnp.concatenate([jnp.where(at, v, 0.0) for at in (tall_lane, flat_lane)], axis=1)
            for v in (coarse, fine)
        ],
        axis=0,
    ).astype(BF16)
    labels = dot(jnp.concatenate([one_hot(tall), one_hot(flat)], axis=1), lanes, (1, 1))
    send(chans + 1, EDGE, labels[:, :width] * 32.0 + labels[:, width:])
    for chan, sent in enumerate(exact_dots(of_seg, ocean)):
        send(chan, cap, sent)
    return stores


def send_kernel(seg, mask, area, dest, row, ocean, sent):
    segs, width = mask.target.shape
    count = area.target.shape[0]
    lines = count // width
    chans = ocean.target.shape[0]
    first = chans * segs
    found = seg.get()[...]
    member = one_hot(iota((segs, count), 0) == found)
    sea = dot(member, mask.get()[...].astype(F32).astype(BF16), (0, 0))
    sent[first : first + count, :] = area.get()[...] * sea
    flat = [
        index[:, line * width : (line + 1) * width].astype(F32)
        for index in (dest.get()[...], found, row.get()[...])
        for line in range(lines)
    ]
    rest = sent.shape[0] - first - count - len(flat)
    sent[first + count :, :] = jnp.concatenate(flat + [jnp.zeros((rest, width), F32)], axis=0)
    values = ocean.get()
    for chan in range(chans):
        sent[chan * segs : (chan + 1) * segs, :] = values[chan]


def pack_kernel(sizes, count, chans, half, sent, out, staged, out_sems):
    width = sent.shape[1]
    lines = count // width
    rest = -(-3 * lines // 16) * 16
    segs = (sent.shape[0] - count - rest) // chans
    first = chans * segs + count

    def vector(index):
        at = first + index * lines
        pieces = [sent[at + line : at + line + 1, :] for line in range(lines)]
        return jnp.concatenate(pieces, axis=1).astype(jnp.int32)

    ocean = [sent[chan * segs : (chan + 1) * segs, :] for chan in range(chans)]
    weight = sent[chans * segs : first, :]
    indices = [vector(index) for index in range(3)]
    for copy in pack(sizes, half[0], *indices, ocean, weight, out, staged, out_sems):
        copy.wait()


def edge_lane(takes, width, high):
    def lane(line):
        at, first = jnp.full(line.shape, -1, jnp.int32), 0
        for index, take in enumerate(takes):
            inside = (line >= first) & (line < first + take)
            start = index * width + (width - take if high else 0)
            at = jnp.where(inside, start + line - first, at)
            first += take
        return at

    return lane


def strip_lane(first, chans, width):
    def lane(line):
        at, place = jnp.full(line.shape, -1, jnp.int32), line % STRIP
        start = (first + line // STRIP) * width
        low = (place >= ITERS) & (place < 3 * ITERS)
        high = (place >= 3 * ITERS) & (place < 5 * ITERS)
        at = jnp.where(low, start + place - ITERS, at)
        at = jnp.where(high, start + width + place - 5 * ITERS, at)
        return jnp.where(line < chans * STRIP, at, -1)

    return lane


def fill_strip(own, left, right, first, chans, take):
    pieces = []
    gap = [jnp.zeros((ITERS - take, own.shape[1]), F32)] if take < ITERS else []
    for chan in range(chans):
        beside = slice(first + chan * take, first + (chan + 1) * take)
        inner = slice(chan * STRIP + ITERS, (chan + 1) * STRIP - ITERS)
        pieces += gap + [left[beside, 0, :], own[inner, :], right[beside, 0, :]] + gap
    pieces.append(jnp.zeros((own.shape[0] - chans * STRIP, own.shape[1]), F32))
    return jnp.concatenate(pieces, axis=0)


def edge_columns(pieces, outputs):
    width = pieces[0][0].shape[1]
    length = outputs[0][0].shape[-1]
    tail = length - sum(piece.shape[0] for piece in pieces[0])
    whole = jnp.concatenate(
        [jnp.concatenate([*piece, jnp.zeros((tail, width), F32)], axis=0) for piece in pieces],
        axis=1,
    )
    rows = []
    for ref, lane in outputs:
        shape = (-(-ref.shape[0] // EDGE) * EDGE, whole.shape[1])
        rows.append(iota(shape, 1) == lane(iota(shape, 0)))
    select = one_hot(jnp.concatenate([row.astype(jnp.int32) for row in rows], axis=0) > 0)
    top, middle, bottom = split3(whole)
    edges = dot(select, bottom, (1, 1)) + dot(select, middle, (1, 1))
    edges = edges + dot(select, top, (1, 1))
    first = 0
    for ref, _ in outputs:
        ref[...] = edges[first : first + ref.shape[0]].reshape(ref.shape)
        first += -(-ref.shape[0] // EDGE) * EDGE


def first_columns_kernel(before, after, atm, diff, low, high, own):
    chans, _, width = atm.target.shape
    bodies = [ref.get()[chan] for ref in (atm, diff) for chan in range(chans)]
    takes = [1] * chans + [ITERS - 1] * chans
    pieces = [(before[i], body, after[i]) for i, body in enumerate(bodies)]
    edge_columns(
        pieces,
        [
            (low, edge_lane(takes, width, False)),
            (high, edge_lane(takes, width, True)),
            (own, strip_lane(chans, chans, width)),
        ],
    )


def columns_kernel(before, body, after, low, high, own):
    chans, _, width = body.shape
    pieces = [(before[i], body[i], after[i]) for i in range(chans)]
    edge_columns(
        pieces,
        [
            (low, edge_lane([ITERS] * chans, width, False)),
            (high, edge_lane([ITERS] * chans, width, True)),
            (own, strip_lane(0, chans, width)),
        ],
    )


def beside_rows(x):
    rows = x.shape[0]
    return pltpu.roll(x, rows - 1, 0) + pltpu.roll(x, 1, 0)


def beside_columns(x):
    width = x.shape[1]
    return pltpu.roll(x, width - 1, 1), pltpu.roll(x, 1, 1)


def beside_body(body, side=None):
    rows, width = body.shape
    lane = iota(body.shape, 1)
    east, west = beside_columns(body)
    east = jnp.where(lane == width - 1, 0.0 if side is None else side, east)
    west = jnp.where(lane == 0, 0.0 if side is None else side, west)
    return beside_rows(body) + east + west


def smooth_kernel(cap, before, after, left, right, atm, dest, seg, table, seg_select, held, sems):
    chans, rows, width = atm.target.shape
    segs, slots = held.shape
    target = dest.get()[...]
    slot = target * cap + positions(target, slots // cap)
    place = one_hot(iota((slots, target.shape[1]), 0) == slot)
    member = one_hot(iota((segs, target.shape[1]), 0) == seg.get()[...])
    held[...] = dot(member, place, (1, 1)).astype(BF16)
    stores = [pltpu.make_async_copy(held, seg_select, sems.at[0])]
    stores[0].start()
    sides = nearest_columns(left, right, width, chans)
    state = atm.get()
    parts = []
    for chan in range(chans):
        body = jnp.concatenate([before[chan], state[chan], after[chan]], axis=0)
        side = sides[: body.shape[0], chan * width : (chan + 1) * width]
        parts.append(split3((0.5 * body + 0.125 * beside_body(body, side))[EDGE : EDGE + rows]))
    table[...] = jnp.concatenate([p[level] for level in (2, 1, 0) for p in parts], axis=1)
    for store in stores:
        store.wait()


def nearest_columns(left, right, width, chans):
    edges = jnp.concatenate([left[:EDGE, 0, :], right[:EDGE, 0, :]], axis=0)
    shape = (6 * EDGE, chans * width)
    which, lane = iota(shape, 0), iota(shape, 1)
    line = which % (2 * EDGE)
    at = jnp.where(line < EDGE, line * width, (line - EDGE) * width + width - 1)
    select = one_hot((lane == at) & (line % EDGE < chans))
    return dot(jnp.concatenate(split3(edges), axis=0), select, (0, 0))


def flux_kernel(cap, ocn_count, mirrored, half, incoming, table, *rest):
    out, label_rows, staged, sems = rest[-4:]
    incoming = incoming if mirrored else incoming.get()
    owners, _, width = incoming.shape
    chans = staged.shape[1] // cap
    rows = table.shape[0]
    across = ocn_count // 2
    base = (1 - half[0] if mirrored else half[0]) * across
    groups = 4
    each = owners // groups
    stores = []
    label_rows[...] = incoming[:, (chans + 1) * cap, :]
    for group in range(groups):
        part_of = slice(group * each, (group + 1) * each)

        def part(index):
            piece = incoming[part_of, index * cap : (index + 1) * cap, :]
            return piece.reshape(each * cap, width)

        labels = incoming[part_of, (chans + 1) * cap :, :]
        labels = jnp.concatenate(
            [labels[i, :, j : j + 1] for i in range(each) for j in range(cap // EDGE)], axis=0
        ).astype(jnp.int32)
        select = one_hot(iota((each * cap, rows), 1) == labels)
        found = dot(select, table[...])
        pieces = [found[:, i * width : (i + 1) * width] for i in range(3 * chans)]
        air = [(pieces[i] + pieces[chans + i]) + pieces[2 * chans + i] for i in range(chans)]
        wind_east = air[1] - part(1)
        wind_north = air[2] - part(2)
        wind_speed = jnp.sqrt(wind_east * wind_east + wind_north * wind_north + 0.5)
        temp_gap = part(0) - air[0]
        factor = 1.0 + 0.5 * jnp.tanh(temp_gap / wind_speed)
        common = part(3) * factor * wind_speed
        for index, value in enumerate((0.8 * temp_gap, 0.6 * wind_east, 0.6 * wind_north)):
            staged[part_of, index * cap : (index + 1) * cap, :] = (common * value).reshape(
                each, cap, width
            )
        for line in range(group * each // across, (group + 1) * each // across):
            store = pltpu.make_async_copy(
                staged.at[pl.ds(line * across, across)],
                out.at[pl.ds(line * ocn_count + base, across)],
                sems.at[line],
            )
            store.start()
            stores.append(store)
    for store in stores:
        store.wait()


def forced_kernel(
    cap, ocn_count, half, own_labels, mirror_labels, weighted, atm, forced, top, bottom, held, sems
):
    owners, width = own_labels.shape
    devices = 2 * owners
    chans, rows, _ = forced.shape
    slots = devices * cap
    log = cap.bit_length() - 1
    across = ocn_count // 2
    loads = [
        pltpu.make_async_copy(
            weighted.at[pl.ds(line * ocn_count + base * across, across)],
            held.at[pl.ds(side * owners + line * across, across)],
            sems.at[side * (owners // across) + line],
        )
        for side, base in enumerate((half[0], 1 - half[0]))
        for line in range(owners // across)
    ]
    for load in loads:
        load.start()
    labels = jnp.concatenate([own_labels[...], mirror_labels[...]], axis=0).astype(jnp.int32)
    spread = one_hot(iota((width, slots), 0) == (iota((width, slots), 1) & (cap - 1)) + FLAT)
    coarse = dot(lax.shift_right_logical(labels, 5).astype(F32).astype(BF16), spread)
    fine = dot((labels & 31).astype(F32).astype(BF16), spread)
    owner = lax.shift_right_logical(iota((devices, slots), 1), log)
    label = jnp.where(owner == iota((devices, slots), 0), coarse * 32.0 + fine, 0.0)
    label = jnp.sum(label, axis=0, keepdims=True).astype(jnp.int32)
    select = one_hot(iota((rows, slots), 0) == label)
    state = atm.get()
    for load in loads:
        load.wait()
    values = [
        held[:, chan * cap : (chan + 1) * cap, :].reshape(slots, width) for chan in range(chans)
    ]
    for chan in range(chans):
        (air_sum,) = exact_dots(select, [values[chan]])
        result = state[chan] + air_sum if chan == 0 else state[chan] - air_sum
        forced[chan] = result
        top[chan] = result[:EDGE]
        bottom[chan] = result[-EDGE:]


def diffuse_kernel(
    forced, before, after, diff_own, diff_left, diff_right, diff_before, diff_after, diff,
    out, diff_strip, staged, sems,
):
    chans, rows, width = forced.shape
    diff_strip[...] = fill_strip(diff_own, diff_left, diff_right, chans, chans, ITERS - 1)
    stores = []
    for chan in range(chans):
        body = jnp.concatenate([before[chan], forced[chan], after[chan]], axis=0)
        body_diff = [diff_before[chans + chan], diff.get()[chan], diff_after[chans + chan]]
        body_diff = jnp.concatenate(body_diff, axis=0)
        for _ in range(ITERS):
            body = body + body_diff * (beside_body(body) - 4.0 * body)
        staged[chan] = body[EDGE : EDGE + rows]
        stores.append(pltpu.make_async_copy(staged.at[chan], out.at[chan], sems.at[chan]))
        stores[-1].start()
    for store in stores:
        store.wait()


def finish_kernel(
    cap, returned, own, left, right, diff_strip, seg_select, inner, ocean_flux, atm_next,
    flux_staged, staged, sems,
):
    devices, _, width = returned.shape
    chans, rows, _ = staged.shape
    stores = []

    def send(source, target):
        stores.append(pltpu.make_async_copy(source, target, sems.at[len(stores)]))
        stores[-1].start()

    values = [
        returned[:, chan * cap : (chan + 1) * cap, :].reshape(devices * cap, width)
        for chan in range(chans)
    ]
    select = seg_select.get()[...]
    for chan in range(chans):
        (flux_staged[chan],) = exact_dots(select, [values[chan]])
    send(flux_staged, ocean_flux)
    state = fill_strip(own, left, right, 0, chans, ITERS)
    spread = diff_strip[...]
    for _ in range(ITERS):
        east, west = beside_columns(state)
        state = state + spread * ((beside_rows(state) + east + west) - 4.0 * state)
    lines = state.shape[0]
    shape = (3 * lines, chans * width)
    which, lane = iota(shape, 0) % lines, iota(shape, 1)
    place, start = which % STRIP, which // STRIP * width
    low = (place >= ITERS) & (place < 2 * ITERS) & (lane == start + place - ITERS)
    high = (place >= 4 * ITERS) & (place < 5 * ITERS)
    high = high & (lane == start + width + place - 5 * ITERS)
    select = one_hot((which < chans * STRIP) & (low | high))
    edges = dot(jnp.concatenate(split3(state), axis=0), select, (0, 0))
    lane = iota((rows, width), 1)
    outer = (lane < ITERS) | (lane >= width - ITERS)
    middle = inner.get()
    for chan in range(chans):
        edge = edges[EDGE : EDGE + rows, chan * width : (chan + 1) * width]
        staged[chan] = jnp.where(outer, edge, middle[chan])
        send(staged.at[chan], atm_next.at[chan])
    for store in stores:
        store.wait()


def shift(axis, low_edge, high_edge):
    count = lax.axis_size(axis)
    forward = [(i, i + 1) for i in range(count - 1)]
    backward = [(target, source) for source, target in forward]
    return lax.ppermute(high_edge, axis, forward), lax.ppermute(low_edge, axis, backward)


def per_device(atm, diff, ocean, mask, area, seg, dest, row):
    atm_count, ocn_count = lax.axis_size("atm"), lax.axis_size("ocn")
    devices = atm_count * ocn_count
    rows, chans, width = atm.shape
    count = seg.shape[0]
    segs = ocean.shape[0]
    cap = max(2, 2 * count // devices)
    slots = devices * cap
    atm = jnp.transpose(atm, (1, 0, 2))
    diff = jnp.transpose(diff, (1, 0, 2))
    ocean = jnp.transpose(ocean, (1, 0, 2))

    def shape(*dims, dtype=F32):
        return jax.ShapeDtypeStruct(dims, dtype)

    hbm, fast = pltpu.HBM, pl.BlockSpec(memory_space=pltpu.VMEM)
    slow = pl.BlockSpec(memory_space=hbm)
    dest, seg, row = dest.reshape(1, count), seg.reshape(1, count), row.reshape(1, count)
    across = ocn_count // 2
    owners = devices // 2
    half = (lax.axis_index("ocn") // across).astype(jnp.int32).reshape(1)
    halves = [
        [i * ocn_count + side * across + j for i in range(atm_count) for j in range(across)]
        for side in range(2)
    ]
    mirror = [(j, (j + across) % ocn_count) for j in range(ocn_count)]
    sizes = (devices, ocn_count, cap)
    packed = (owners, (chans + 1) * cap + EDGE, width)
    lines_sent = chans * segs + count + -(-3 * count // width // 16) * 16

    def exchange(x):
        return lax.all_to_all(
            x, BOTH, split_axis=0, concat_axis=0, tiled=True, axis_index_groups=halves
        )

    sent = call(
        send_kernel,
        shape(lines_sent, width),
        (seg, mask, area, dest, row, ocean),
        late=(0, 1, 2, 3, 4, 5),
        cost=COST_SEND,
    )
    received = lax.ppermute(sent, "ocn", mirror)

    def packing(sent, cost, *ahead):
        return call(
            functools.partial(pack_kernel, sizes, count, chans),
            hbm(packed, F32),
            (half, sent),
            smem=(0,),
            after=ahead,
            outs=slow,
            scratch=[pltpu.VMEM(packed, F32), pltpu.SemaphoreType.DMA((chans + 2,))],
            cost=cost,
        )

    first = jnp.concatenate([atm[:, :EDGE], diff[:, :EDGE]], axis=0)
    final = jnp.concatenate([atm[:, -EDGE:], diff[:, -EDGE:]], axis=0)
    before, after = shift("atm", first, final)
    own_packed = packing(sent, COST_OWN)
    own_incoming = exchange(own_packed)
    long = -(-(rows + 2 * EDGE) // 128) * 128

    edge = shape(chans * ITERS, 1, long)

    def lines(columns):
        return shape(-(-columns // EDGE) * EDGE, long)

    low, high, diff_own = call(
        first_columns_kernel,
        (edge, edge, lines(chans * STRIP)),
        (before, after, atm, diff),
        late=(2, 3),
        after=(own_packed,),
        cost=COST_FIRST,
    )
    left, right = shift("ocn", low, high)
    mirror_packed = packing(received, COST_MIRROR, diff_own)
    mirror_incoming = exchange(mirror_packed)

    table, seg_select = call(
        functools.partial(smooth_kernel, cap),
        (pltpu.VMEM((rows, 3 * chans * width), BF16), hbm((segs, slots), BF16)),
        (before, after, left, right, atm, dest, seg),
        late=(4, 5, 6),
        after=(mirror_packed,),
        outs=(fast, slow),
        cost=COST_SMOOTH,
        scratch=[pltpu.VMEM((segs, slots), BF16), pltpu.SemaphoreType.DMA((1,))],
    )

    def flux(incoming, mirrored, begun):
        return call(
            functools.partial(flux_kernel, cap, ocn_count, mirrored),
            (
                hbm((devices, chans * cap, width), F32),
                shape(owners, width),
            ),
            (half, incoming, table, *begun),
            smem=(0,),
            late=() if mirrored else (1,),
            outs=(slow, fast),
            scratch=[
                pltpu.VMEM((owners, chans * cap, width), F32),
                pltpu.SemaphoreType.DMA((atm_count,)),
            ],
            aliases={3: 0} if begun else {},
        )

    begun, own_labels = flux(own_incoming, False, ())
    weighted, mirror_labels = flux(mirror_incoming, True, (begun,))
    returned = lax.all_to_all(weighted, BOTH, split_axis=0, concat_axis=0, tiled=True)
    forced, top, bottom = call(
        functools.partial(forced_kernel, cap, ocn_count),
        (
            pltpu.VMEM((chans, rows, width), F32),
            shape(chans, EDGE, width),
            shape(chans, EDGE, width),
        ),
        (half, own_labels, mirror_labels, weighted, atm),
        smem=(0,),
        plain=(3,),
        late=(4,),
        scratch=[
            pltpu.VMEM((devices, chans * cap, width), F32),
            pltpu.SemaphoreType.DMA((2 * atm_count,)),
        ],
    )
    forced_before, forced_after = shift("atm", top, bottom)
    forced_low, forced_high, forced_own = call(
        columns_kernel,
        (edge, edge, lines(chans * STRIP)),
        (forced_before, forced, forced_after),
    )
    forced_left, forced_right = shift("ocn", forced_low, forced_high)
    inner, diff_strip = call(
        diffuse_kernel,
        (hbm((chans, rows, width), F32), lines(chans * STRIP)),
        (forced, forced_before, forced_after, diff_own, left, right, before, after, diff),
        late=(8,),
        outs=(slow, fast),
        scratch=[pltpu.VMEM((chans, rows, width), F32), pltpu.SemaphoreType.DMA((chans,))],
    )
    ocean_flux, atm_next = call(
        functools.partial(finish_kernel, cap),
        (hbm((chans, segs, width), F32), hbm((chans, rows, width), F32)),
        (returned, forced_own, forced_left, forced_right, diff_strip, seg_select, inner),
        late=(5, 6),
        outs=(slow, slow),
        scratch=[
            pltpu.VMEM((chans, segs, width), F32),
            pltpu.VMEM((chans, rows, width), F32),
            pltpu.SemaphoreType.DMA((1 + chans,)),
        ],
    )
    return jnp.transpose(atm_next, (1, 0, 2)), jnp.transpose(ocean_flux, (1, 0, 2))


def solution(mesh):
    placed = (
        P("atm", None, "ocn"),
        P("atm", None, "ocn"),
        P(BOTH, None, None),
        P(BOTH, None),
        P(BOTH, None),
        P(BOTH),
        P(BOTH, None),
        P(BOTH),
    )
    return jax.shard_map(
        per_device,
        mesh=mesh,
        in_specs=placed,
        out_specs=(P("atm", None, "ocn"), P(BOTH, None, None)),
        check_vma=False,
    )
```
